128 devices in a mesh: row: 16 (over y_lo, x, core), col: 8 (over z, y_hi).
Axes of the slice: x: 4, y: 4 (y_hi: 2, y_lo: 2; y = y_hi * 2 + y_lo), z: 4, core: 2. Of those that a mesh axis runs over, the one named last changes fastest.
Arguments:
- passages: float32 [131072, 1024], P('row', 'col'), may hold values from -6 to 6
- list_ids: int32 [131072], P('row'), may hold values from 0 to 4095
- code_ids: int32 [131072, 64], P('row', 'col'), may hold values from 0 to 255
- old_centroids: float32 [4096, 1024], P('row', 'col'), may hold values from -6 to 6
- old_codebook: float32 [256, 1024], P('row', 'col'), may hold values from -5 to 5
Outputs:
- centroids: float32 [4096, 1024], P('row', 'col')
- codebook: float32 [256, 1024], P('row', 'col')
- distortion: float32 [131072], P('row')
The draws below stay inside these ranges and needn't reach their ends.
All inputs are finite; a program needn't handle non-finite values.
Results may differ from the reference program's by a relative error of at most 0.000082.
Values sent between devices are 32-bit elements; how exact they have to be, the bound alone decides.
No kernel may reach another device: no remote copies, remote signals or barrier semaphores. Data moves between devices by JAX's collectives and lax.ppermute only.
A program may use at most 64 MiB of HBM per device.

```python
import jax
import jax.numpy as jnp

D = 1024
LISTS = 4096
SUBS = 64
CODES = 256
ROWS = 131072
SUB_DIM = 16
LIST_PRIOR = 32
CODE_PRIOR = 512


def place_ends(entries, stream_key, smallest, largest):
    shape = entries.shape
    index_at = [jax.random.randint(jax.random.fold_in(stream_key, axis), (), 0, shape[axis]) for axis in range(len(shape))]
    entries = entries.at[tuple(index_at)].set(smallest)
    longest = shape.index(max(shape))
    index_at[longest] = (index_at[longest] + 1) % shape[longest]
    return entries.at[tuple(index_at)].set(largest)


def shard_levels(rng, dims, pieces, least, high):
    level, own = 1.0, jax.random.fold_in(rng, 6)
    for position, parts in pieces:
        heights = jnp.exp(jax.random.uniform(jax.random.fold_in(own, position), (parts,), jnp.float32, least / len(pieces), high / len(pieces)))
        level = level * jnp.repeat(heights, dims[position] // parts).reshape([-1 if axis == position else 1 for axis in range(len(dims))])
    return level


def scatter_about(rng, shape, width, reach, shards=(), held_as=jnp.bfloat16):
    entries = jax.random.normal(rng, shape, jnp.float32) * width
    if len(shards) > 0:
        entries = shard_levels(rng, shape, shards, -0.22, 0.18) * entries
    return jnp.clip(entries, min=-reach, max=reach).astype(held_as)


def setup_inputs(seed: int = 0) -> dict:
    splits = jax.random.split(jax.random.key(seed), 6)
    return {
        "passages": scatter_about(splits[0], (ROWS, D), 1.0, 6.0, ((0, 16), (1, 8)), jnp.float32),
        "list_ids": place_ends(jax.random.randint(splits[1], (ROWS,), 0, LISTS), jax.random.fold_in(splits[1], 1), 0, LISTS - 1).astype(jnp.int32),
        "code_ids": place_ends(jax.random.randint(splits[2], (ROWS, SUBS), 0, CODES), jax.random.fold_in(splits[2], 1), 0, CODES - 1).astype(jnp.int32),
        "old_centroids": scatter_about(splits[3], (LISTS, D), 1.0, 6.0, ((0, 16), (1, 8)), jnp.float32),
        "old_codebook": scatter_about(splits[4], (CODES, D), 0.7, 5.0, ((0, 16), (1, 8)), jnp.float32),
    }


def reference(passages, list_ids, code_ids, old_centroids, old_codebook):
    list_sums = jax.ops.segment_sum(passages, list_ids, LISTS)
    list_counts = jax.ops.segment_sum(jnp.ones((ROWS,), jnp.float32), list_ids, LISTS)
    centroids = (list_sums + LIST_PRIOR * old_centroids) / (list_counts[:, None] + LIST_PRIOR)
    residual = passages - centroids[list_ids]
    split = residual.reshape(ROWS, SUBS, SUB_DIM)

    def one_sub(vectors, ids):
        sums = jax.ops.segment_sum(vectors, ids, CODES)
        counts = jax.ops.segment_sum(jnp.ones((ROWS,), jnp.float32), ids, CODES)
        return sums, counts

    sums, counts = jax.vmap(one_sub, in_axes=(1, 1))(split, code_ids)
    code_sums = jnp.transpose(sums, (1, 0, 2))
    code_counts = jnp.transpose(counts, (1, 0))
    old_split = old_codebook.reshape(CODES, SUBS, SUB_DIM)
    book = (code_sums + CODE_PRIOR * old_split) / (code_counts[:, :, None] + CODE_PRIOR)
    codebook = book.reshape(CODES, D)
    recon = book[code_ids, jnp.arange(SUBS, dtype=jnp.int32)[None, :]]
    distortion = jnp.sum((split - recon) ** 2, axis=(1, 2)) / D
    return centroids, codebook, distortion
```

```python
import functools
import jax
import jax.numpy as jnp
from jax import lax
from jax.experimental import pallas as pl
from jax.experimental.pallas import tpu as pltpu

from jax.sharding import PartitionSpec as P

HIGH = lax.Precision.HIGHEST
D = 1024
LANES = 128
SUB_DIM = 16
NACC = 8
SLAB = 8


def sums_kernel(core_ref, ids_ref, idv_ref, codes_ref, x_ref, keep_ref, send_ref, lcnt, ccnt, *accs):
    step = pl.program_id(0)
    block = x_ref.shape[0]
    lists = accs[0].shape[0]
    pieces = keep_ref.shape[0]
    owned = lists // (2 * pieces)

    @pl.when(step == 0)
    def _():
        zero = jnp.zeros((256, LANES), jnp.float32)

        @pl.loop(0, lists // 256)
        def _(i):
            for acc in accs:
                acc[pl.ds(i * 256, 256), :] = zero

        lcnt[...] = jnp.zeros_like(lcnt)
        ccnt[...] = jnp.zeros_like(ccnt)

    base = step * block

    @pl.loop(0, block // UNROLL1)
    def _(i):
        r0 = i * UNROLL1
        for u in range(0, UNROLL1, NACC):
            ids = [ids_ref[base + r0 + u + j] for j in range(NACC)]
            old = [accs[j][pl.ds(ids[j], 1), :] for j in range(NACC)]
            new = [x_ref[pl.ds(r0 + u + j, 1), :] for j in range(NACC)]
            for j in range(NACC):
                accs[j][pl.ds(ids[j], 1), :] = old[j] + new[j]

    nhi = lists // LANES
    hi_iota = lax.broadcasted_iota(jnp.int32, (nhi, LANES), 0)
    lo_iota = lax.broadcasted_iota(jnp.int32, (LANES, LANES), 0)
    his, los = [], []
    for t in range(block // LANES):
        row = idv_ref[pl.ds(step * (block // LANES) + t, 1), :]
        his.append((row // LANES == hi_iota).astype(jnp.bfloat16))
        los.append((row % LANES == lo_iota).astype(jnp.bfloat16))
    nt = (((1,), (1,)), ((), ()))
    lcnt[...] += lax.dot_general(
        jnp.concatenate(his, 1), jnp.concatenate(los, 1), nt, preferred_element_type=jnp.float32
    )
    dig = lax.broadcasted_iota(jnp.int32, (SUB_DIM, block), 0)
    his, los = [], []
    for m in range(codes_ref.shape[0]):
        row = codes_ref[pl.ds(m, 1), :]
        his.append((row // SUB_DIM == dig).astype(jnp.bfloat16))
        los.append((row % SUB_DIM == dig).astype(jnp.bfloat16))
    ccnt[...] += lax.dot_general(
        jnp.concatenate(his, 0), jnp.concatenate(los, 0), nt, preferred_element_type=jnp.float32
    )

    @pl.when(step == pl.num_programs(0) - 1)
    def _():
        core = core_ref[0]
        cc = ccnt[...]
        r = lax.broadcasted_iota(jnp.int32, cc.shape, 0) // SUB_DIM
        c = lax.broadcasted_iota(jnp.int32, cc.shape, 1) // SUB_DIM
        cc = jnp.where(r == c, cc, 0.0)
        crow = cc[0:SUB_DIM, :]
        for m in range(1, codes_ref.shape[0]):
            crow = crow + cc[m * SUB_DIM:(m + 1) * SUB_DIM, :]
        ccnt[0:SUB_DIM, :] = crow
        for out, par in ((keep_ref, core), (send_ref, 1 - core)):
            @pl.loop(0, pieces)
            def _(k):
                owner = 2 * k + par
                start = pl.multiple_of(owner * owned, owned)
                total = accs[0][pl.ds(start, owned), :]
                for acc in accs[1:]:
                    total = total + acc[pl.ds(start, owned), :]
                out[k, 0:owned, :] = total
                out[k, pl.ds(owned, SLAB), :] = jnp.concatenate(
                    [
                        lcnt[pl.ds(owner * (owned // LANES), owned // LANES), :],
                        ccnt[pl.ds(owner, 1), :],
                        jnp.zeros((SLAB - owned // LANES - 1, LANES), jnp.float32),
                    ],
                    0,
                )


UNROLL1 = 32


def list_sums(core, ids, codes_t, x, pieces, lists, block=1024):
    rows, width = x.shape
    owned = lists // (2 * pieces)
    out = jax.ShapeDtypeStruct((pieces, owned + SLAB, width), jnp.float32)
    full = pl.BlockSpec((pieces, owned + SLAB, width), lambda i: (0, 0, 0))
    return pl.pallas_call(
        sums_kernel,
        grid=(rows // block,),
        in_specs=[
            pl.BlockSpec(memory_space=pltpu.SMEM),
            pl.BlockSpec(memory_space=pltpu.SMEM),
            pl.BlockSpec((rows // LANES, LANES), lambda i: (0, 0)),
            pl.BlockSpec((codes_t.shape[0], block), lambda i: (0, i)),
            pl.BlockSpec((block, width), lambda i: (i, 0)),
        ],
        out_specs=[full, full],
        out_shape=[out, out],
        scratch_shapes=[
            pltpu.VMEM((lists // LANES, LANES), jnp.float32),
            pltpu.VMEM((LANES, LANES), jnp.float32),
        ]
        + [pltpu.VMEM((lists, width), jnp.float32)] * NACC,
        compiler_params=pltpu.CompilerParams(vmem_limit_bytes=48 * 2**20),
        name="list_sums",
    )(core, ids, ids.reshape(rows // LANES, LANES), codes_t, x)


def centroid_kernel(prior, part_ref, old_ref, cent_ref, copies_ref, tail_ref):
    owned = old_ref.shape[0]
    total = part_ref[0]
    for k in range(1, part_ref.shape[0]):
        total = total + part_ref[k]
    eye = (
        lax.broadcasted_iota(jnp.int32, (LANES, LANES), 0)
        == lax.broadcasted_iota(jnp.int32, (LANES, LANES), 1)
    )
    for h in range(owned // LANES):
        row = total[owned + h : owned + h + 1, :]
        col = jnp.sum(jnp.where(eye, row, 0.0), axis=1, keepdims=True)
        sl = slice(h * LANES, (h + 1) * LANES)
        cent = (total[sl, :] + prior * old_ref[sl, :]) / (col + prior)
        cent_ref[sl, :] = cent
        for k in range(copies_ref.shape[0]):
            copies_ref[k, sl, :] = cent
    tail_ref[...] = total[owned:, :]


def new_centroids(parts, old, prior):
    n, _, width = parts.shape
    return pl.pallas_call(
        functools.partial(centroid_kernel, prior),
        out_shape=[
            jax.ShapeDtypeStruct(old.shape, jnp.float32),
            jax.ShapeDtypeStruct((n,) + old.shape, jnp.float32),
            jax.ShapeDtypeStruct((SLAB, width), jnp.float32),
        ],
        compiler_params=pltpu.CompilerParams(vmem_limit_bytes=32 * 2**20),
        name="centroids",
    )(parts, old)


UNROLL3 = 32


def resid_kernel(core_ref, ids_ref, codes_ref, x_ref, own_ref, other_ref, rest_ref, sums_ref, table, got):
    step = pl.program_id(0)
    block = x_ref.shape[0]
    pieces, owned, _ = own_ref.shape
    subs = codes_ref.shape[0]
    codes = sums_ref.shape[0]

    @pl.when(step == 0)
    def _():
        core = core_ref[0]
        for k in range(pieces):
            table[pl.ds(pl.multiple_of((2 * k + core) * owned, owned), owned), :] = own_ref[k]
            table[pl.ds(pl.multiple_of((2 * k + 1 - core) * owned, owned), owned), :] = other_ref[k]
        sums_ref[...] = jnp.zeros_like(sums_ref)

    base = step * block

    @pl.loop(0, block // UNROLL3)
    def _(i):
        r0 = i * UNROLL3
        rows = [table[pl.ds(ids_ref[base + r0 + j], 1), :] for j in range(UNROLL3)]
        for j in range(UNROLL3):
            got[pl.ds(r0 + j, 1), :] = rows[j]

    res = x_ref[...] - got[...]
    rest_ref[...] = res.T
    hi = res.astype(jnp.bfloat16)
    lo = (res - hi.astype(jnp.float32)).astype(jnp.bfloat16)
    both = jnp.concatenate([hi, lo], 1)
    lane_sub = lax.broadcasted_iota(jnp.int32, (codes, LANES), 1) // SUB_DIM
    label = lax.broadcasted_iota(jnp.int32, (codes, block), 0)
    total = sums_ref[...]
    for m in range(subs):
        hot = (codes_ref[pl.ds(m, 1), :] == label).astype(jnp.bfloat16)
        part = jnp.dot(hot, both, preferred_element_type=jnp.float32)
        total = total + jnp.where(lane_sub == m, part[:, :LANES] + part[:, LANES:], 0.0)
    sums_ref[...] = total


def residuals(core, ids, codes_t, x, own, other, codes, block=1024):
    rows, width = x.shape
    pieces, owned, _ = own.shape
    whole = pl.BlockSpec(own.shape, lambda i: (0, 0, 0))
    return pl.pallas_call(
        resid_kernel,
        grid=(rows // block,),
        in_specs=[
            pl.BlockSpec(memory_space=pltpu.SMEM),
            pl.BlockSpec(memory_space=pltpu.SMEM),
            pl.BlockSpec((codes_t.shape[0], block), lambda i: (0, i)),
            pl.BlockSpec((block, width), lambda i: (i, 0)),
            whole,
            whole,
        ],
        out_specs=[
            pl.BlockSpec((width, block), lambda i: (0, i)),
            pl.BlockSpec((codes, width), lambda i: (0, 0)),
        ],
        out_shape=[
            jax.ShapeDtypeStruct((width, rows), jnp.float32),
            jax.ShapeDtypeStruct((codes, width), jnp.float32),
        ],
        scratch_shapes=[
            pltpu.VMEM((2 * pieces * owned, width), jnp.float32),
            pltpu.VMEM((block, width), jnp.float32),
        ],
        compiler_params=pltpu.CompilerParams(vmem_limit_bytes=48 * 2**20),
        name="residuals",
    )(core, ids, codes_t, x, own, other)


def errors_kernel(book_ref, codes_ref, rest_ref, out_ref, table):
    width, block = rest_ref.shape
    subs = codes_ref.shape[0]

    @pl.when(pl.program_id(0) == 0)
    def _():
        table[...] = book_ref[...].T

    for t in range(block // LANES):
        cols = slice(t * LANES, (t + 1) * LANES)
        acc = jnp.zeros((8, LANES), jnp.float32)
        for m in range(subs):
            idx = jnp.broadcast_to(codes_ref[m:m + 1, cols], (8, LANES))
            low = idx % LANES
            first = idx < LANES
            for g in range(SUB_DIM // 8):
                f = slice(m * SUB_DIM + g * 8, m * SUB_DIM + g * 8 + 8)
                a = jnp.take_along_axis(table[f, 0:LANES], low, axis=1)
                b = jnp.take_along_axis(table[f, LANES:2 * LANES], low, axis=1)
                d = rest_ref[f, cols] - jnp.where(first, a, b)
                acc = acc + d * d
        out_ref[t:t + 1, :] = jnp.sum(acc, axis=0, keepdims=True)


def errors(book, codes_t, rest, block=1024):
    width, rows = rest.shape
    return pl.pallas_call(
        errors_kernel,
        grid=(rows // block,),
        in_specs=[
            pl.BlockSpec(book.shape, lambda i: (0, 0)),
            pl.BlockSpec((codes_t.shape[0], block), lambda i: (0, i)),
            pl.BlockSpec((width, block), lambda i: (0, i)),
        ],
        out_specs=pl.BlockSpec((block // LANES, LANES), lambda i: (i, 0)),
        out_shape=jax.ShapeDtypeStruct((rows // LANES, LANES), jnp.float32),
        scratch_shapes=[pltpu.VMEM((width, book.shape[0]), jnp.float32)],
        compiler_params=pltpu.CompilerParams(vmem_limit_bytes=48 * 2**20),
        name="errors",
    )(book, codes_t, rest)


def book_kernel(prior, part_ref, tail_ref, old_ref, book_ref, copies_ref):
    total = part_ref[0]
    for k in range(1, part_ref.shape[0]):
        total = total + part_ref[k]
    shape = total.shape
    row = jnp.broadcast_to(tail_ref[2:3, :], shape)
    lane = lax.broadcasted_iota(jnp.int32, shape, 1)
    code = lax.broadcasted_iota(jnp.int32, shape, 0)
    picked = jnp.where(lane % SUB_DIM == code, row, 0.0)
    r = lax.broadcasted_iota(jnp.int32, (LANES, LANES), 0) // SUB_DIM
    c = lax.broadcasted_iota(jnp.int32, (LANES, LANES), 1) // SUB_DIM
    ones = (r == c).astype(jnp.float32)
    counts = jnp.dot(picked, ones, precision=HIGH, preferred_element_type=jnp.float32)
    book = (total + prior * old_ref[...]) / (counts + prior)
    book_ref[...] = book
    for k in range(copies_ref.shape[0]):
        copies_ref[k] = book


def new_codebook(parts, tail, old, prior):
    return pl.pallas_call(
        functools.partial(book_kernel, prior),
        out_shape=[
            jax.ShapeDtypeStruct(old.shape, jnp.float32),
            jax.ShapeDtypeStruct(parts.shape, jnp.float32),
        ],
        name="codebook",
    )(parts, tail, old)


def swap(x, axis, n, bit):
    return lax.ppermute(x, axis, [(i, i ^ bit) for i in range(n)])


def local(passages, list_ids, code_ids, old_centroids, old_codebook):
    rows, width = passages.shape
    n_row = lax.axis_size("row")
    n_col = lax.axis_size("col")
    total = rows * n_row
    owned_lists = old_centroids.shape[0]
    owned_codes = old_codebook.shape[0]
    lists = owned_lists * n_row
    codes = owned_codes * n_row
    list_prior = float(total // lists)
    code_prior = float(total // codes)
    pieces = n_row // 2
    same_core = [[2 * k + c for k in range(pieces)] for c in range(2)]
    core = (lax.axis_index("row") % 2).astype(jnp.int32).reshape(1)
    codes_t = code_ids.T

    keep, send = list_sums(core, list_ids, codes_t, passages, pieces, lists)
    pair = keep + swap(send, "row", n_row, 1)
    parts = lax.all_to_all(pair, "row", 0, 0, axis_index_groups=same_core, tiled=True)
    centroids, copies, tail = new_centroids(parts, old_centroids, list_prior)
    own = lax.all_to_all(copies, "row", 0, 0, axis_index_groups=same_core, tiled=True)
    other = swap(own, "row", n_row, 1)
    rest, sums = residuals(core, list_ids, codes_t, passages, own, other, codes)
    parts = lax.all_to_all(sums.reshape(n_row, owned_codes, width), "row", 0, 0, tiled=True)
    codebook, copies = new_codebook(parts, tail, old_codebook, code_prior)
    book = lax.all_to_all(copies, "row", 0, 0, tiled=True).reshape(codes, width)
    err = errors(book, codes_t, rest)
    bit = 1
    while bit < n_col:
        err = err + swap(err, "col", n_col, bit)
        bit *= 2
    return centroids, codebook, err.reshape(rows) / D


def solution(mesh):
    in_specs = (P("row", "col"), P("row"), P("row", "col"), P("row", "col"), P("row", "col"))
    out_specs = (P("row", "col"), P("row", "col"), P("row"))
    return jax.shard_map(local, mesh=mesh, in_specs=in_specs, out_specs=out_specs, check_vma=False)
```

```python
import functools
import jax
import jax.numpy as jnp
from jax import lax
from jax.experimental import pallas as pl
from jax.experimental.pallas import tpu as pltpu

from jax.sharding import PartitionSpec as P

HIGH = lax.Precision.HIGHEST
D = 1024
LANES = 128
SUB_DIM = 16
NACC = 8
SLAB = 8
RBLOCK = 512
ETILE = 1024
VLIM = 20 * 2**20


def sums_kernel(core_ref, ids_hbm, idv_hbm, codes_hbm, x_hbm, keep_ref, send_ref, ids, idv, codes_ref, x_ref, lcnt, ccnt, sems, *accs):
    rows, _ = x_ref.shape
    lists = accs[0].shape[0]
    pieces = keep_ref.shape[0]
    owned = lists // (2 * pieces)
    subs = codes_ref.shape[0]
    nchunk = sems.shape[0] - 3
    chunk = rows // nchunk

    def part(c):
        here = pl.ds(c * chunk, chunk)
        return pltpu.make_async_copy(x_hbm.at[here, :], x_ref.at[here, :], sems.at[c])

    fetch_ids = pltpu.make_async_copy(ids_hbm, ids, sems.at[nchunk])
    fetch_idv = pltpu.make_async_copy(idv_hbm, idv, sems.at[nchunk + 1])
    fetch_codes = pltpu.make_async_copy(codes_hbm, codes_ref, sems.at[nchunk + 2])
    fetch_ids.start()
    part(0).start()
    fetch_idv.start()
    fetch_codes.start()
    for c in range(1, nchunk):
        part(c).start()

    zero = jnp.zeros((ZROWS, LANES), jnp.float32)

    @pl.loop(0, lists // ZROWS)
    def _(i):
        for acc in accs:
            acc[pl.ds(pl.multiple_of(i * ZROWS, ZROWS), ZROWS), :] = zero

    lcnt[...] = jnp.zeros_like(lcnt)
    ccnt[...] = jnp.zeros_like(ccnt)
    fetch_idv.wait()
    fetch_codes.wait()
    fetch_ids.wait()
    nhi = lists // LANES
    nt = (((1,), (1,)), ((), ()))

    def counts(start):
        hi_iota = lax.broadcasted_iota(jnp.int32, (nhi, LANES), 0)
        lo_iota = lax.broadcasted_iota(jnp.int32, (LANES, LANES), 0)
        his, los = [], []
        group = idv[pl.ds(pl.multiple_of(start // LANES, CBLOCK // LANES), CBLOCK // LANES), :]
        for t in range(CBLOCK // LANES):
            row = group[t : t + 1, :]
            his.append((lax.shift_right_logical(row, 7) == hi_iota).astype(jnp.bfloat16))
            los.append(((row & (LANES - 1)) == lo_iota).astype(jnp.bfloat16))
        lcnt[...] += lax.dot_general(
            jnp.concatenate(his, 1), jnp.concatenate(los, 1), nt, preferred_element_type=jnp.float32
        )
        dig = lax.broadcasted_iota(jnp.int32, (SUB_DIM, CBLOCK), 0)
        his, los = [], []
        for m in range(subs):
            row = codes_ref[pl.ds(m, 1), pl.ds(start, CBLOCK)]
            his.append((lax.shift_right_logical(row, 4) == dig).astype(jnp.bfloat16))
            los.append(((row & (SUB_DIM - 1)) == dig).astype(jnp.bfloat16))
        ccnt[...] += lax.dot_general(
            jnp.concatenate(his, 0), jnp.concatenate(los, 0), nt, preferred_element_type=jnp.float32
        )

    def scatter(start):
        for u in range(0, CBLOCK, NACC):
            row = [ids.at[pl.ds(u + j, rows - CBLOCK + 1)][start] for j in range(NACC)]
            old = [accs[j][pl.ds(row[j], 1), :] for j in range(NACC)]
            new = [x_ref[pl.ds(start + u + j, 1), :] for j in range(NACC)]
            for j in range(NACC):
                accs[j][pl.ds(row[j], 1), :] = old[j] + new[j]

    @pl.loop(0, nchunk)
    def _(c):
        part(c).wait()

        @pl.loop(0, chunk // CBLOCK)
        def _(i):
            start = pl.multiple_of(c * chunk + i * CBLOCK, CBLOCK)
            scatter(start)
            counts(start)

    cc = ccnt[...]
    r = lax.broadcasted_iota(jnp.int32, cc.shape, 0) // SUB_DIM
    c = lax.broadcasted_iota(jnp.int32, cc.shape, 1) // SUB_DIM
    cc = jnp.where(r == c, cc, 0.0)
    crow = cc[0:SUB_DIM, :]
    for m in range(1, subs):
        crow = crow + cc[m * SUB_DIM:(m + 1) * SUB_DIM, :]
    ccnt[0:SUB_DIM, :] = crow
    core = core_ref[0]
    for out, par in ((send_ref, 1 - core), (keep_ref, core)):
        @pl.loop(0, pieces)
        def _(k):
            owner = 2 * k + par
            start = pl.multiple_of(owner * owned, owned)
            total = accs[0][pl.ds(start, owned), :]
            for acc in accs[1:]:
                total = total + acc[pl.ds(start, owned), :]
            out[k, 0:owned, :] = total
            out[k, pl.ds(owned, SLAB), :] = jnp.concatenate(
                [
                    lcnt[pl.ds(owner * (owned // LANES), owned // LANES), :],
                    ccnt[pl.ds(owner, 1), :],
                    jnp.zeros((SLAB - owned // LANES - 1, LANES), jnp.float32),
                ],
                0,
            )


CBLOCK = 1024
ZROWS = 64
NCHUNK = 8


def list_sums(core, ids, codes_t, x, pieces, lists):
    rows, width = x.shape
    owned = lists // (2 * pieces)
    out = jax.ShapeDtypeStruct((pieces, owned + SLAB, width), jnp.float32)
    hbm = pl.BlockSpec(memory_space=pl.ANY)
    vmem = pl.BlockSpec(memory_space=pltpu.VMEM)
    return pl.pallas_call(
        sums_kernel,
        in_specs=[pl.BlockSpec(memory_space=pltpu.SMEM)] + [hbm] * 4,
        out_specs=[vmem, vmem],
        out_shape=[out, out],
        scratch_shapes=[
            pltpu.SMEM((rows,), jnp.int32),
            pltpu.VMEM((rows // LANES, LANES), jnp.int32),
            pltpu.VMEM(codes_t.shape, jnp.int32),
            pltpu.VMEM((rows, width), jnp.float32),
            pltpu.VMEM((lists // LANES, LANES), jnp.float32),
            pltpu.VMEM((LANES, LANES), jnp.float32),
            pltpu.SemaphoreType.DMA((NCHUNK + 3,)),
        ]
        + [pltpu.VMEM((lists, width), jnp.float32)] * NACC,
        compiler_params=pltpu.CompilerParams(vmem_limit_bytes=60 * 2**20),
        name="list_sums",
    )(core, ids, ids.reshape(rows // LANES, LANES), codes_t, x)


def centroid_kernel(prior, part_ref, old_ref, cent_ref, copies_ref, tail_ref):
    owned = old_ref.shape[0]
    total = part_ref[0]
    for k in range(1, part_ref.shape[0]):
        total = total + part_ref[k]
    eye = (
        lax.broadcasted_iota(jnp.int32, (LANES, LANES), 0)
        == lax.broadcasted_iota(jnp.int32, (LANES, LANES), 1)
    )
    for h in range(owned // LANES):
        row = total[owned + h : owned + h + 1, :]
        col = jnp.sum(jnp.where(eye, row, 0.0), axis=1, keepdims=True)
        sl = slice(h * LANES, (h + 1) * LANES)
        cent = (total[sl, :] + prior * old_ref[sl, :]) / (col + prior)
        cent_ref[sl, :] = cent
        for k in range(copies_ref.shape[0]):
            copies_ref[k, sl, :] = cent
    tail_ref[...] = total[owned:, :]


def new_centroids(parts, old, prior):
    n, _, width = parts.shape
    return pl.pallas_call(
        functools.partial(centroid_kernel, prior),
        out_shape=[
            jax.ShapeDtypeStruct(old.shape, jnp.float32),
            jax.ShapeDtypeStruct((n,) + old.shape, jnp.float32),
            jax.ShapeDtypeStruct((SLAB, width), jnp.float32),
        ],
        compiler_params=pltpu.CompilerParams(vmem_limit_bytes=32 * 2**20),
        name="centroids",
    )(parts, old)


NT = (((1,), (1,)), ((), ()))


def resid_kernel(
    core_ref, ids_ref, codes_ref, x_ref, own_ref, other_ref, rest_ref, sums_ref, ids, table, got0, got1, sumst, sem
):
    block = got0.shape[0]
    rows = x_ref.shape[0]
    pieces, owned, _ = own_ref.shape
    subs = codes_ref.shape[0]
    half = sums_ref.shape[0] // 2
    fetch = pltpu.make_async_copy(ids_ref, ids, sem)
    fetch.start()
    core = core_ref[0]
    for k in range(pieces):
        table[pl.ds(pl.multiple_of((2 * k + core) * owned, owned), owned), :] = own_ref[k]
        table[pl.ds(pl.multiple_of((2 * k + 1 - core) * owned, owned), owned), :] = other_ref[k]
    sumst[...] = jnp.zeros_like(sumst)
    fetch.wait()

    def gather(start, got):
        for j in range(block):
            row = ids.at[pl.ds(j, rows - block + 1)][start]
            got[pl.ds(j, 1), :] = table[pl.ds(row, 1), :]

    def work(start, got):
        here = pl.ds(start, block)
        rest = (x_ref[here, :] - got[...]).T
        rest_ref[:, here] = rest
        hi = rest.astype(jnp.bfloat16)
        lo = (rest - hi.astype(jnp.float32)).astype(jnp.bfloat16)
        label = lax.broadcasted_iota(jnp.int32, (half, block), 0)
        for p in range(subs // 2):
            left, right = [], []
            for m in (2 * p, 2 * p + 1):
                code = codes_ref[pl.ds(m, 1), here]
                right.append(((code & (half - 1)) == label).astype(jnp.bfloat16))
                f = slice(m * SUB_DIM, (m + 1) * SUB_DIM)
                both = jnp.concatenate([hi[f], lo[f]], 0)
                top = jnp.broadcast_to((code < half).astype(jnp.bfloat16), both.shape)
                first = both * top
                left += [first, both - first]
            part = lax.dot_general(
                jnp.concatenate(left, 0), jnp.concatenate(right, 0), NT, preferred_element_type=jnp.float32
            )
            for s in range(2):
                f = slice((2 * p + s) * SUB_DIM, (2 * p + s + 1) * SUB_DIM)
                for h in range(2):
                    band = part[(4 * s + 2 * h) * SUB_DIM : (4 * s + 2 * h + 2) * SUB_DIM, s * half : (s + 1) * half]
                    sumst[f, h * half : (h + 1) * half] += band[:SUB_DIM] + band[SUB_DIM:]

    gather(0, got0)

    @pl.loop(0, rows // (2 * block))
    def _(i):
        first = pl.multiple_of(2 * i * block, block)
        second = pl.multiple_of(first + block, block)
        third = pl.multiple_of(jnp.minimum(second + block, rows - block), block)
        gather(second, got1)
        work(first, got0)
        gather(third, got0)
        work(second, got1)

    sums_ref[...] = sumst[...].T


def residuals(core, ids, codes_t, x, own, other, codes, block=RBLOCK):
    rows, width = x.shape
    pieces, owned, _ = own.shape
    vmem = pl.BlockSpec(memory_space=pltpu.VMEM)
    return pl.pallas_call(
        resid_kernel,
        in_specs=[pl.BlockSpec(memory_space=pltpu.SMEM)] + [vmem] * 5,
        out_specs=[vmem, vmem],
        out_shape=[
            jax.ShapeDtypeStruct((width, rows), jnp.float32),
            jax.ShapeDtypeStruct((codes, width), jnp.float32),
        ],
        scratch_shapes=[
            pltpu.SMEM((rows,), jnp.int32),
            pltpu.VMEM((2 * pieces * owned, width), jnp.float32),
            pltpu.VMEM((block, width), jnp.float32),
            pltpu.VMEM((block, width), jnp.float32),
            pltpu.VMEM((width, codes), jnp.float32),
            pltpu.SemaphoreType.DMA(()),
        ],
        compiler_params=pltpu.CompilerParams(vmem_limit_bytes=VLIM),
        name="residuals",
    )(core, ids, codes_t, x, own, other)


def errors_kernel(book_ref, codes_ref, rest_ref, out_ref, table):
    subs, rows = codes_ref.shape
    half = book_ref.shape[0] // 2
    table[...] = book_ref[...].T

    @pl.loop(0, rows // ETILE)
    def _(i):
        sums = []
        for t in range(ETILE // LANES):
            cols = pl.ds(pl.multiple_of(i * ETILE, ETILE) + t * LANES, LANES)
            acc = jnp.zeros((8, LANES), jnp.float32)
            for m in range(subs):
                idx = jnp.broadcast_to(codes_ref[pl.ds(m, 1), cols], (8, LANES))
                low = idx & (half - 1)
                first = idx < half
                for g in range(SUB_DIM // 8):
                    f = slice(m * SUB_DIM + g * 8, m * SUB_DIM + g * 8 + 8)
                    a = jnp.take_along_axis(table[f, 0:half], low, axis=1)
                    b = jnp.take_along_axis(table[f, half:2 * half], low, axis=1)
                    d = rest_ref[f, cols] - jnp.where(first, a, b)
                    acc = acc + d * d
            sums.append(jnp.sum(acc, axis=0, keepdims=True))
        out_ref[pl.ds(pl.multiple_of(i * (ETILE // LANES), ETILE // LANES), ETILE // LANES), :] = jnp.concatenate(sums, 0)


def errors(book, codes_t, rest):
    width, rows = rest.shape
    vmem = pl.BlockSpec(memory_space=pltpu.VMEM)
    return pl.pallas_call(
        errors_kernel,
        in_specs=[vmem] * 3,
        out_specs=vmem,
        out_shape=jax.ShapeDtypeStruct((rows // LANES, LANES), jnp.float32),
        scratch_shapes=[pltpu.VMEM((width, book.shape[0]), jnp.float32)],
        compiler_params=pltpu.CompilerParams(vmem_limit_bytes=VLIM),
        name="errors",
    )(book, codes_t, rest)


def book_kernel(prior, part_ref, tail_ref, old_ref, book_ref, copies_ref):
    total = part_ref[0]
    for k in range(1, part_ref.shape[0]):
        total = total + part_ref[k]
    shape = total.shape
    row = jnp.broadcast_to(tail_ref[2:3, :], shape)
    lane = lax.broadcasted_iota(jnp.int32, shape, 1)
    code = lax.broadcasted_iota(jnp.int32, shape, 0)
    picked = jnp.where(lane % SUB_DIM == code, row, 0.0)
    r = lax.broadcasted_iota(jnp.int32, (LANES, LANES), 0) // SUB_DIM
    c = lax.broadcasted_iota(jnp.int32, (LANES, LANES), 1) // SUB_DIM
    ones = (r == c).astype(jnp.float32)
    counts = jnp.dot(picked, ones, precision=HIGH, preferred_element_type=jnp.float32)
    book = (total + prior * old_ref[...]) / (counts + prior)
    book_ref[...] = book
    for k in range(copies_ref.shape[0]):
        copies_ref[k] = book


def new_codebook(parts, tail, old, prior):
    return pl.pallas_call(
        functools.partial(book_kernel, prior),
        out_shape=[
            jax.ShapeDtypeStruct(old.shape, jnp.float32),
            jax.ShapeDtypeStruct(parts.shape, jnp.float32),
        ],
        name="codebook",
    )(parts, tail, old)


def swap(x, axis, n, bit):
    return lax.ppermute(x, axis, [(i, i ^ bit) for i in range(n)])


def local(passages, list_ids, code_ids, old_centroids, old_codebook):
    rows, width = passages.shape
    n_row = lax.axis_size("row")
    n_col = lax.axis_size("col")
    total = rows * n_row
    owned_lists = old_centroids.shape[0]
    owned_codes = old_codebook.shape[0]
    lists = owned_lists * n_row
    codes = owned_codes * n_row
    list_prior = float(total // lists)
    code_prior = float(total // codes)
    pieces = n_row // 2
    same_core = [[2 * k + c for k in range(pieces)] for c in range(2)]
    core = (lax.axis_index("row") % 2).astype(jnp.int32).reshape(1)
    codes_t = code_ids.T

    keep, send = list_sums(core, list_ids, codes_t, passages, pieces, lists)
    pair = keep + swap(send, "row", n_row, 1)
    parts = lax.all_to_all(pair, "row", 0, 0, axis_index_groups=same_core, tiled=True)
    centroids, copies, tail = new_centroids(parts, old_centroids, list_prior)
    own = lax.all_to_all(copies, "row", 0, 0, axis_index_groups=same_core, tiled=True)
    other = swap(own, "row", n_row, 1)
    rest, sums = residuals(core, list_ids, codes_t, passages, own, other, codes)
    parts = lax.all_to_all(sums.reshape(n_row, owned_codes, width), "row", 0, 0, tiled=True)
    codebook, copies = new_codebook(parts, tail, old_codebook, code_prior)
    book = lax.all_to_all(copies, "row", 0, 0, tiled=True).reshape(codes, width)
    err = errors(book, codes_t, rest)
    bit = 1
    while bit < n_col:
        err = err + swap(err, "col", n_col, bit)
        bit *= 2
    return centroids, codebook, err.reshape(rows) / D


def solution(mesh):
    in_specs = (P("row", "col"), P("row"), P("row", "col"), P("row", "col"), P("row", "col"))
    out_specs = (P("row", "col"), P("row", "col"), P("row"))
    return jax.shard_map(local, mesh=mesh, in_specs=in_specs, out_specs=out_specs, check_vma=False)
```

```python
import functools
import jax
import jax.numpy as jnp
from jax import lax
from jax.experimental import pallas as pl
from jax.experimental.pallas import tpu as pltpu

from jax.sharding import PartitionSpec as P

HIGH = lax.Precision.HIGHEST
D = 1024
LANES = 128
SUB_DIM = 16
NACC = 8
SLAB = 8
K1LIM = 50 * 2**20
SPARE = 5
RBLOCK = 512
EBLOCK = 2048
VLIM = 40 * 2**20


def sums_kernel(core_ref, ids_hbm, idv_hbm, x_hbm, keep_ref, send_ref, ids, idv, x_ref, lcnt, sems, *accs):
    rows, _ = x_ref.shape
    lists = accs[0].shape[0]
    pieces = keep_ref.shape[0]
    owned = lists // (2 * pieces)
    nchunk = sems.shape[0] - 2
    chunk = rows // nchunk

    def part(c):
        here = pl.ds(c * chunk, chunk)
        return pltpu.make_async_copy(x_hbm.at[here, :], x_ref.at[here, :], sems.at[c])

    fetch_ids = pltpu.make_async_copy(ids_hbm, ids, sems.at[nchunk])
    fetch_idv = pltpu.make_async_copy(idv_hbm, idv, sems.at[nchunk + 1])
    fetch_ids.start()
    part(0).start()
    fetch_idv.start()
    for c in range(1, nchunk):
        part(c).start()

    zero = jnp.zeros((ZROWS, LANES), jnp.float32)

    @pl.loop(0, lists // ZROWS)
    def _(i):
        for acc in accs:
            acc[pl.ds(pl.multiple_of(i * ZROWS, ZROWS), ZROWS), :] = zero

    lcnt[...] = jnp.zeros_like(lcnt)
    fetch_idv.wait()
    fetch_ids.wait()
    nhi = lists // LANES
    nt = (((1,), (1,)), ((), ()))

    def counts(start):
        hi_iota = lax.broadcasted_iota(jnp.int32, (nhi, LANES), 0)
        lo_iota = lax.broadcasted_iota(jnp.int32, (LANES, LANES), 0)
        his, los = [], []
        group = idv[pl.ds(pl.multiple_of(start // LANES, CBLOCK // LANES), CBLOCK // LANES), :]
        for t in range(CBLOCK // LANES):
            row = group[t : t + 1, :]
            his.append((lax.shift_right_logical(row, 7) == hi_iota).astype(jnp.bfloat16))
            los.append(((row & (LANES - 1)) == lo_iota).astype(jnp.bfloat16))
        lcnt[...] += lax.dot_general(
            jnp.concatenate(his, 1), jnp.concatenate(los, 1), nt, preferred_element_type=jnp.float32
        )

    def scatter(start):
        for u in range(0, CBLOCK, NACC):
            row = [ids.at[pl.ds(u + j, rows - CBLOCK + 1)][start] for j in range(NACC)]
            old = [accs[j][pl.ds(row[j], 1), :] for j in range(NACC)]
            new = [x_ref[pl.ds(start + u + j, 1), :] for j in range(NACC)]
            for j in range(NACC):
                accs[j][pl.ds(row[j], 1), :] = old[j] + new[j]

    @pl.loop(0, nchunk)
    def _(c):
        part(c).wait()

        @pl.loop(0, chunk // CBLOCK)
        def _(i):
            start = pl.multiple_of(c * chunk + i * CBLOCK, CBLOCK)
            scatter(start)
            counts(start)

    core = core_ref[0]
    for out, par in ((send_ref, 1 - core), (keep_ref, core)):
        @pl.loop(0, pieces)
        def _(k):
            owner = 2 * k + par
            start = pl.multiple_of(owner * owned, owned)
            total = accs[0][pl.ds(start, owned), :]
            for acc in accs[1:]:
                total = total + acc[pl.ds(start, owned), :]
            out[k, 0:owned, :] = total
            out[k, pl.ds(owned, SLAB), :] = jnp.concatenate(
                [
                    lcnt[pl.ds(owner * (owned // LANES), owned // LANES), :],
                    jnp.zeros((SLAB - owned // LANES, LANES), jnp.float32),
                ],
                0,
            )


CBLOCK = 1024
ZROWS = 64
NCHUNK = 8


def list_sums(core, ids, x, pieces, lists):
    rows, width = x.shape
    owned = lists // (2 * pieces)
    out = jax.ShapeDtypeStruct((pieces, owned + SLAB, width), jnp.float32)
    hbm = pl.BlockSpec(memory_space=pltpu.HBM)
    vmem = pl.BlockSpec(memory_space=pltpu.VMEM)
    return pl.pallas_call(
        sums_kernel,
        in_specs=[pl.BlockSpec(memory_space=pltpu.SMEM)] + [hbm] * 3,
        out_specs=[vmem, vmem],
        out_shape=[out, out],
        scratch_shapes=[
            pltpu.SMEM((rows,), jnp.int32),
            pltpu.VMEM((rows // LANES, LANES), jnp.int32),
            pltpu.VMEM((rows, width), jnp.float32),
            pltpu.VMEM((lists // LANES, LANES), jnp.float32),
            pltpu.SemaphoreType.DMA((NCHUNK + 2,)),
        ]
        + [pltpu.VMEM((lists, width), jnp.float32)] * NACC,
        compiler_params=pltpu.CompilerParams(vmem_limit_bytes=K1LIM),
        name="list_sums",
    )(core, ids, ids.reshape(rows // LANES, LANES), x)


def centroid_kernel(prior, part_ref, old_ref, cent_ref, copies_ref):
    owned = old_ref.shape[0]
    total = part_ref[0]
    for k in range(1, part_ref.shape[0]):
        total = total + part_ref[k]
    eye = (
        lax.broadcasted_iota(jnp.int32, (LANES, LANES), 0)
        == lax.broadcasted_iota(jnp.int32, (LANES, LANES), 1)
    )
    for h in range(owned // LANES):
        row = total[owned + h : owned + h + 1, :]
        col = jnp.sum(jnp.where(eye, row, 0.0), axis=1, keepdims=True)
        sl = slice(h * LANES, (h + 1) * LANES)
        cent = (total[sl, :] + prior * old_ref[sl, :]) / (col + prior)
        cent_ref[sl, :] = cent
        for k in range(copies_ref.shape[0]):
            copies_ref[k, sl, :] = cent


def new_centroids(parts, old, prior):
    n = parts.shape[0]
    return pl.pallas_call(
        functools.partial(centroid_kernel, prior),
        out_shape=[
            jax.ShapeDtypeStruct(old.shape, jnp.float32),
            jax.ShapeDtypeStruct((n,) + old.shape, jnp.float32),
        ],
        compiler_params=pltpu.CompilerParams(vmem_limit_bytes=16 * 2**20),
        name="centroids",
    )(parts, old)


NT = (((1,), (1,)), ((), ()))


def resid_kernel(
    core_ref, ids_ref, codes_ref, x_ref, own_ref, other_ref, rest_hbm, sums_ref, ids, table, got0, got1, sumst, ccnt, rest_ref, sem, out_sems
):
    block = got0.shape[0]
    rows = x_ref.shape[0]
    pieces, owned, _ = own_ref.shape
    subs = codes_ref.shape[0]
    owners, slab, _ = sums_ref.shape
    each = slab - SLAB
    half = owners * each // 2
    fetch = pltpu.make_async_copy(ids_ref, ids, sem)
    fetch.start()
    core = core_ref[0]
    for k in range(pieces):
        table[pl.ds(pl.multiple_of((2 * k + core) * owned, owned), owned), :] = own_ref[k]
        table[pl.ds(pl.multiple_of((2 * k + 1 - core) * owned, owned), owned), :] = other_ref[k]
    sumst[...] = jnp.zeros_like(sumst)
    ccnt[...] = jnp.zeros_like(ccnt)
    fetch.wait()

    def gather(start, got):
        for j in range(block):
            row = ids.at[pl.ds(j, rows - block + 1)][start]
            got[pl.ds(j, 1), :] = table[pl.ds(row, 1), :]

    def work(start, got):
        here = pl.ds(start, block)
        rest = (x_ref[here, :] - got[...]).T
        rest_ref[:, here] = rest
        hi = rest.astype(jnp.bfloat16)
        lo = (rest - hi.astype(jnp.float32)).astype(jnp.bfloat16)
        label = lax.broadcasted_iota(jnp.int32, (half, block), 0)
        digit = lax.broadcasted_iota(jnp.int32, (SUB_DIM, block), 0)
        left, right = [], []
        for m in range(subs):
            code = codes_ref[pl.ds(m, 1), here]
            left.append((lax.shift_right_logical(code, 4) == digit).astype(jnp.bfloat16))
            right.append(((code & (SUB_DIM - 1)) == digit).astype(jnp.bfloat16))
        ccnt[...] += lax.dot_general(
            jnp.concatenate(left, 0), jnp.concatenate(right, 0), NT, preferred_element_type=jnp.float32
        )
        for p in range(subs // 2):
            left, right = [], []
            for m in (2 * p, 2 * p + 1):
                code = codes_ref[pl.ds(m, 1), here]
                right.append(((code & (half - 1)) == label).astype(jnp.bfloat16))
                f = slice(m * SUB_DIM, (m + 1) * SUB_DIM)
                both = jnp.concatenate([hi[f], lo[f]], 0)
                top = jnp.broadcast_to((code < half).astype(jnp.bfloat16), both.shape)
                first = both * top
                left += [first, both - first]
            part = lax.dot_general(
                jnp.concatenate(left, 0), jnp.concatenate(right, 0), NT, preferred_element_type=jnp.float32
            )
            for s in range(2):
                f = slice((2 * p + s) * SUB_DIM, (2 * p + s + 1) * SUB_DIM)
                for h in range(2):
                    band = part[(4 * s + 2 * h) * SUB_DIM : (4 * s + 2 * h + 2) * SUB_DIM, s * half : (s + 1) * half]
                    sumst[f, h * half : (h + 1) * half] += band[:SUB_DIM] + band[SUB_DIM:]

    def store(start):
        here = pl.ds(start, block)
        return pltpu.make_async_copy(rest_ref.at[:, here], rest_hbm.at[0, :, here], out_sems.at[start // block])

    gather(0, got0)

    @pl.loop(0, rows // (2 * block))
    def _(i):
        first = pl.multiple_of(2 * i * block, block)
        second = pl.multiple_of(first + block, block)
        third = pl.multiple_of(jnp.minimum(second + block, rows - block), block)
        gather(second, got1)
        work(first, got0)
        gather(third, got0)
        work(second, got1)
        store(first).start()
        store(second).start()

    total = sumst[...].T
    cc = ccnt[...]
    r = lax.broadcasted_iota(jnp.int32, cc.shape, 0) // SUB_DIM
    c = lax.broadcasted_iota(jnp.int32, cc.shape, 1) // SUB_DIM
    cc = jnp.where(r == c, cc, 0.0)
    crow = cc[0:SUB_DIM, :]
    for m in range(1, subs):
        crow = crow + cc[m * SUB_DIM : (m + 1) * SUB_DIM, :]
    fill = jnp.zeros((SLAB - 1, LANES), jnp.float32)
    for o in range(owners):
        sums_ref[o, 0:each, :] = total[o * each : (o + 1) * each, :]
        sums_ref[o, each:slab, :] = jnp.concatenate([crow[o : o + 1, :], fill], 0)
    for c in range(rows // block):
        store(c * block).wait()


def residuals(core, ids, codes_t, x, own, other, owners, codes, block=RBLOCK):
    rows, width = x.shape
    pieces, owned, _ = own.shape
    vmem = pl.BlockSpec(memory_space=pltpu.VMEM)
    return pl.pallas_call(
        resid_kernel,
        in_specs=[pl.BlockSpec(memory_space=pltpu.SMEM)] + [vmem] * 5,
        out_specs=[pl.BlockSpec(memory_space=pltpu.HBM), vmem],
        out_shape=[
            jax.ShapeDtypeStruct((SPARE, width, rows), jnp.float32),
            jax.ShapeDtypeStruct((owners, codes // owners + SLAB, width), jnp.float32),
        ],
        scratch_shapes=[
            pltpu.SMEM((rows,), jnp.int32),
            pltpu.VMEM((2 * pieces * owned, width), jnp.float32),
            pltpu.VMEM((block, width), jnp.float32),
            pltpu.VMEM((block, width), jnp.float32),
            pltpu.VMEM((width, codes), jnp.float32),
            pltpu.VMEM((LANES, LANES), jnp.float32),
            pltpu.VMEM((width, rows), jnp.float32),
            pltpu.SemaphoreType.DMA(()),
            pltpu.SemaphoreType.DMA((rows // block,)),
        ],
        compiler_params=pltpu.CompilerParams(vmem_limit_bytes=VLIM),
        name="residuals",
    )(core, ids, codes_t, x, own, other)


def errors_kernel(book_ref, codes_ref, rest_ref, out_ref, table):
    subs = codes_ref.shape[0]
    half = book_ref.shape[0] // 2

    @pl.when(pl.program_id(0) == 0)
    def _():
        table[...] = book_ref[...].T

    for t in range(rest_ref.shape[2] // LANES):
        cols = slice(t * LANES, (t + 1) * LANES)
        acc = jnp.zeros((8, LANES), jnp.float32)
        for m in range(subs):
            idx = jnp.broadcast_to(codes_ref[m : m + 1, cols], (8, LANES))
            low = idx & (half - 1)
            first = idx < half
            for g in range(SUB_DIM // 8):
                f = slice(m * SUB_DIM + g * 8, m * SUB_DIM + g * 8 + 8)
                a = jnp.take_along_axis(table[f, 0:half], low, axis=1)
                b = jnp.take_along_axis(table[f, half : 2 * half], low, axis=1)
                d = rest_ref[0, f, cols] - jnp.where(first, a, b)
                acc = acc + d * d
        row = jnp.sum(acc, axis=0, keepdims=True)
        for k in range(out_ref.shape[0]):
            out_ref[k, t : t + 1, :] = row


def errors(book, codes_t, rest, copies, block=EBLOCK):
    _, width, rows = rest.shape
    return pl.pallas_call(
        errors_kernel,
        grid=(rows // block,),
        in_specs=[
            pl.BlockSpec(book.shape, lambda i: (0, 0)),
            pl.BlockSpec((codes_t.shape[0], block), lambda i: (0, i)),
            pl.BlockSpec((1, width, block), lambda i: (0, 0, i)),
        ],
        out_specs=pl.BlockSpec((copies, block // LANES, LANES), lambda i: (0, i, 0)),
        out_shape=jax.ShapeDtypeStruct((copies, rows // LANES, LANES), jnp.float32),
        scratch_shapes=[pltpu.VMEM((width, book.shape[0]), jnp.float32)],
        compiler_params=pltpu.CompilerParams(vmem_limit_bytes=58 * 2**20),
        name="errors",
    )(book, codes_t, rest)


def book_kernel(prior, part_ref, old_ref, book_ref, copies_ref):
    total = part_ref[0]
    for k in range(1, part_ref.shape[0]):
        total = total + part_ref[k]
    shape = old_ref.shape
    row = jnp.broadcast_to(total[shape[0] : shape[0] + 1, :], shape)
    lane = lax.broadcasted_iota(jnp.int32, shape, 1)
    code = lax.broadcasted_iota(jnp.int32, shape, 0)
    picked = jnp.where(lane % SUB_DIM == code, row, 0.0)
    r = lax.broadcasted_iota(jnp.int32, (LANES, LANES), 0) // SUB_DIM
    c = lax.broadcasted_iota(jnp.int32, (LANES, LANES), 1) // SUB_DIM
    ones = (r == c).astype(jnp.float32)
    counts = jnp.dot(picked, ones, precision=HIGH, preferred_element_type=jnp.float32)
    book = (total[: shape[0], :] + prior * old_ref[...]) / (counts + prior)
    book_ref[...] = book
    for k in range(copies_ref.shape[0]):
        copies_ref[k] = book


def new_codebook(parts, old, prior):
    return pl.pallas_call(
        functools.partial(book_kernel, prior),
        out_shape=[
            jax.ShapeDtypeStruct(old.shape, jnp.float32),
            jax.ShapeDtypeStruct((parts.shape[0],) + old.shape, jnp.float32),
        ],
        compiler_params=pltpu.CompilerParams(vmem_limit_bytes=4 * 2**20),
        name="codebook",
    )(parts, old)


def swap(x, axis, n, bit):
    return lax.ppermute(x, axis, [(i, i ^ bit) for i in range(n)])


def local(passages, list_ids, code_ids, old_centroids, old_codebook):
    rows, width = passages.shape
    n_row = lax.axis_size("row")
    n_col = lax.axis_size("col")
    total = rows * n_row
    owned_lists = old_centroids.shape[0]
    owned_codes = old_codebook.shape[0]
    lists = owned_lists * n_row
    codes = owned_codes * n_row
    list_prior = float(total // lists)
    code_prior = float(total // codes)
    pieces = n_row // 2
    same_core = [[2 * k + c for k in range(pieces)] for c in range(2)]
    core = (lax.axis_index("row") % 2).astype(jnp.int32).reshape(1)
    codes_t = code_ids.T

    keep, send = list_sums(core, list_ids, passages, pieces, lists)
    pair = keep + swap(send, "row", n_row, 1)
    parts = lax.all_to_all(pair, "row", 0, 0, axis_index_groups=same_core, tiled=True)
    centroids, copies = new_centroids(parts, old_centroids, list_prior)
    own = lax.all_to_all(copies, "row", 0, 0, axis_index_groups=same_core, tiled=True)
    other = swap(own, "row", n_row, 1)
    rest, sums = residuals(core, list_ids, codes_t, passages, own, other, n_row, codes)
    parts = lax.all_to_all(sums, "row", 0, 0, tiled=True)
    codebook, copies = new_codebook(parts, old_codebook, code_prior)
    book = lax.all_to_all(copies, "row", 0, 0, tiled=True).reshape(codes, width)
    err = errors(book, codes_t, rest, n_col)
    err = lax.all_to_all(err, "col", 0, 0, tiled=True)
    return centroids, codebook, jnp.sum(err, axis=0).reshape(rows) / D


def solution(mesh):
    in_specs = (P("row", "col"), P("row"), P("row", "col"), P("row", "col"), P("row", "col"))
    out_specs = (P("row", "col"), P("row", "col"), P("row"))
    return jax.shard_map(local, mesh=mesh, in_specs=in_specs, out_specs=out_specs, check_vma=False)
```

```python
import functools
import jax
import jax.numpy as jnp
from jax import lax
from jax.experimental import pallas as pl
from jax.experimental.pallas import tpu as pltpu

from jax.sharding import PartitionSpec as P

HIGH = lax.Precision.HIGHEST
D = 1024
LANES = 128
SUB_DIM = 16
NACC = 8
SLAB = 8
K1LIM = 50 * 2**20
SPARE = 5
RBLOCK = 512
EBLOCK = 512
EPAIRS = 2
VLIM = 40 * 2**20


def sums_kernel(core_ref, ids_hbm, idv_hbm, x_hbm, keep_ref, send_ref, ids, idv, x_ref, lcnt, sems, *accs):
    rows, _ = x_ref.shape
    lists = accs[0].shape[0]
    pieces = keep_ref.shape[0]
    owned = lists // (2 * pieces)
    nchunk = sems.shape[0] - 2
    chunk = rows // nchunk

    def part(c):
        here = pl.ds(c * chunk, chunk)
        return pltpu.make_async_copy(x_hbm.at[here, :], x_ref.at[here, :], sems.at[c])

    fetch_ids = pltpu.make_async_copy(ids_hbm, ids, sems.at[nchunk])
    fetch_idv = pltpu.make_async_copy(idv_hbm, idv, sems.at[nchunk + 1])
    fetch_ids.start()
    part(0).start()
    fetch_idv.start()
    for c in range(1, nchunk):
        part(c).start()

    fetch_idv.wait()
    nhi = lists // LANES
    nt = (((1,), (1,)), ((), ()))

    def counts():
        hi_iota = lax.broadcasted_iota(jnp.int32, (nhi, LANES), 0)
        lo_iota = lax.broadcasted_iota(jnp.int32, (LANES, LANES), 0)
        his, los = [], []
        for t in range(rows // LANES):
            row = idv[t : t + 1, :]
            his.append((lax.shift_right_logical(row, 7) == hi_iota).astype(jnp.bfloat16))
            los.append(((row & (LANES - 1)) == lo_iota).astype(jnp.bfloat16))
        lcnt[...] = lax.dot_general(
            jnp.concatenate(his, 1), jnp.concatenate(los, 1), nt, preferred_element_type=jnp.float32
        )

    def scatter(start):
        for u in range(0, CBLOCK, NACC):
            row = [ids.at[pl.ds(u + j, rows - CBLOCK + 1)][start] for j in range(NACC)]
            old = [accs[j][pl.ds(row[j], 1), :] for j in range(NACC)]
            new = [x_ref[pl.ds(start + u + j, 1), :] for j in range(NACC)]
            for j in range(NACC):
                accs[j][pl.ds(row[j], 1), :] = old[j] + new[j]

    for acc in accs:
        acc[...] = jnp.zeros_like(acc)
    counts()
    fetch_ids.wait()

    @pl.loop(0, nchunk)
    def _(c):
        part(c).wait()

        @pl.loop(0, chunk // CBLOCK)
        def _(i):
            start = pl.multiple_of(c * chunk + i * CBLOCK, CBLOCK)
            scatter(start)

    core = core_ref[0]
    for out, par in ((send_ref, 1 - core), (keep_ref, core)):
        @pl.loop(0, pieces)
        def _(k):
            owner = 2 * k + par
            start = pl.multiple_of(owner * owned, owned)
            total = accs[0][pl.ds(start, owned), :]
            for acc in accs[1:]:
                total = total + acc[pl.ds(start, owned), :]
            out[k, 0:owned, :] = total
            out[k, pl.ds(owned, SLAB), :] = jnp.concatenate(
                [
                    lcnt[pl.ds(owner * (owned // LANES), owned // LANES), :],
                    jnp.zeros((SLAB - owned // LANES, LANES), jnp.float32),
                ],
                0,
            )


CBLOCK = 1024
NCHUNK = 8


def list_sums(core, ids, x, pieces, lists):
    rows, width = x.shape
    owned = lists // (2 * pieces)
    out = jax.ShapeDtypeStruct((pieces, owned + SLAB, width), jnp.float32)
    hbm = pl.BlockSpec(memory_space=pltpu.HBM)
    vmem = pl.BlockSpec(memory_space=pltpu.VMEM)
    return pl.pallas_call(
        sums_kernel,
        in_specs=[pl.BlockSpec(memory_space=pltpu.SMEM)] + [hbm] * 3,
        out_specs=[vmem, vmem],
        out_shape=[out, out],
        scratch_shapes=[
            pltpu.SMEM((rows,), jnp.int32),
            pltpu.VMEM((rows // LANES, LANES), jnp.int32),
            pltpu.VMEM((rows, width), jnp.float32),
            pltpu.VMEM((lists // LANES, LANES), jnp.float32),
            pltpu.SemaphoreType.DMA((NCHUNK + 2,)),
        ]
        + [pltpu.VMEM((lists, width), jnp.float32)] * NACC,
        compiler_params=pltpu.CompilerParams(vmem_limit_bytes=K1LIM),
        name="list_sums",
    )(core, ids, ids.reshape(rows // LANES, LANES), x)


def centroid_kernel(prior, part_ref, old_ref, cent_ref, copies_ref):
    owned = old_ref.shape[0]
    total = part_ref[0]
    for k in range(1, part_ref.shape[0]):
        total = total + part_ref[k]
    eye = (
        lax.broadcasted_iota(jnp.int32, (LANES, LANES), 0)
        == lax.broadcasted_iota(jnp.int32, (LANES, LANES), 1)
    )
    for h in range(owned // LANES):
        row = total[owned + h : owned + h + 1, :]
        col = jnp.sum(jnp.where(eye, row, 0.0), axis=1, keepdims=True)
        sl = slice(h * LANES, (h + 1) * LANES)
        cent = (total[sl, :] + prior * old_ref[sl, :]) / (col + prior)
        cent_ref[sl, :] = cent
        for k in range(copies_ref.shape[0]):
            copies_ref[k, sl, :] = cent


def new_centroids(parts, old, prior):
    n = parts.shape[0]
    return pl.pallas_call(
        functools.partial(centroid_kernel, prior),
        out_shape=[
            jax.ShapeDtypeStruct(old.shape, jnp.float32),
            jax.ShapeDtypeStruct((n,) + old.shape, jnp.float32),
        ],
        compiler_params=pltpu.CompilerParams(vmem_limit_bytes=16 * 2**20),
        name="centroids",
    )(parts, old)


NT = (((1,), (1,)), ((), ()))


def resid_kernel(
    core_ref, ids_ref, codes_ref, x_ref, own_ref, other_ref, rest_hbm, sums_ref, ids, table, got0, got1, sumst, ccnt, rest_ref, sem, out_sems
):
    block = got0.shape[0]
    rows = x_ref.shape[0]
    pieces, owned, _ = own_ref.shape
    subs = codes_ref.shape[0]
    owners, slab, _ = sums_ref.shape
    each = slab - SLAB
    half = owners * each // 2
    fetch = pltpu.make_async_copy(ids_ref, ids, sem)
    fetch.start()
    core = core_ref[0]
    for k in range(pieces):
        table[pl.ds(pl.multiple_of((2 * k + core) * owned, owned), owned), :] = own_ref[k]
        table[pl.ds(pl.multiple_of((2 * k + 1 - core) * owned, owned), owned), :] = other_ref[k]
    sumst[...] = jnp.zeros_like(sumst)
    ccnt[...] = jnp.zeros_like(ccnt)
    fetch.wait()

    sublane = lax.broadcasted_iota(jnp.int32, (8, LANES), 0)

    def gather(start, got):
        for g in range(0, block, 8):
            tile = None
            for j in range(8):
                row = ids.at[pl.ds(g + j, rows - block + 1)][start]
                line = jnp.broadcast_to(table[pl.ds(row, 1), :], (8, LANES))
                tile = line if j == 0 else jnp.where(sublane == j, line, tile)
            got[g : g + 8, :] = tile

    def work(start, got):
        here = pl.ds(start, block)
        rest = (x_ref[here, :] - got[...]).T
        rest_ref[:, here] = rest
        hi = rest.astype(jnp.bfloat16)
        lo = (rest - hi.astype(jnp.float32)).astype(jnp.bfloat16)
        label = lax.broadcasted_iota(jnp.int32, (half, block), 0)
        digit = lax.broadcasted_iota(jnp.int32, (SUB_DIM, block), 0)
        left, right = [], []
        for m in range(subs):
            code = codes_ref[pl.ds(m, 1), here]
            left.append((lax.shift_right_logical(code, 4) == digit).astype(jnp.bfloat16))
            right.append(((code & (SUB_DIM - 1)) == digit).astype(jnp.bfloat16))
        ccnt[...] += lax.dot_general(
            jnp.concatenate(left, 0), jnp.concatenate(right, 0), NT, preferred_element_type=jnp.float32
        )
        for p in range(subs // 2):
            left, right = [], []
            for m in (2 * p, 2 * p + 1):
                code = codes_ref[pl.ds(m, 1), here]
                right.append(((code & (half - 1)) == label).astype(jnp.bfloat16))
                f = slice(m * SUB_DIM, (m + 1) * SUB_DIM)
                both = jnp.concatenate([hi[f], lo[f]], 0)
                top = jnp.broadcast_to((code < half).astype(jnp.bfloat16), both.shape)
                first = both * top
                left += [first, both - first]
            part = lax.dot_general(
                jnp.concatenate(left, 0), jnp.concatenate(right, 0), NT, preferred_element_type=jnp.float32
            )
            for s in range(2):
                f = slice((2 * p + s) * SUB_DIM, (2 * p + s + 1) * SUB_DIM)
                for h in range(2):
                    band = part[(4 * s + 2 * h) * SUB_DIM : (4 * s + 2 * h + 2) * SUB_DIM, s * half : (s + 1) * half]
                    sumst[f, h * half : (h + 1) * half] += band[:SUB_DIM] + band[SUB_DIM:]

    def store(start):
        here = pl.ds(start, block)
        return pltpu.make_async_copy(rest_ref.at[:, here], rest_hbm.at[0, :, here], out_sems.at[start // block])

    gather(0, got0)

    @pl.loop(0, rows // (2 * block))
    def _(i):
        first = pl.multiple_of(2 * i * block, block)
        second = pl.multiple_of(first + block, block)
        third = pl.multiple_of(jnp.minimum(second + block, rows - block), block)
        gather(second, got1)
        work(first, got0)
        gather(third, got0)
        work(second, got1)
        store(first).start()
        store(second).start()

    total = sumst[...].T
    cc = ccnt[...]
    r = lax.broadcasted_iota(jnp.int32, cc.shape, 0) // SUB_DIM
    c = lax.broadcasted_iota(jnp.int32, cc.shape, 1) // SUB_DIM
    cc = jnp.where(r == c, cc, 0.0)
    crow = cc[0:SUB_DIM, :]
    for m in range(1, subs):
        crow = crow + cc[m * SUB_DIM : (m + 1) * SUB_DIM, :]
    fill = jnp.zeros((SLAB - 1, LANES), jnp.float32)
    for o in range(owners):
        sums_ref[o, 0:each, :] = total[o * each : (o + 1) * each, :]
        sums_ref[o, each:slab, :] = jnp.concatenate([crow[o : o + 1, :], fill], 0)
    for c in range(rows // block):
        store(c * block).wait()


def residuals(core, ids, codes_t, x, own, other, owners, codes, block=RBLOCK):
    rows, width = x.shape
    pieces, owned, _ = own.shape
    vmem = pl.BlockSpec(memory_space=pltpu.VMEM)
    return pl.pallas_call(
        resid_kernel,
        in_specs=[pl.BlockSpec(memory_space=pltpu.SMEM)] + [vmem] * 5,
        out_specs=[pl.BlockSpec(memory_space=pltpu.HBM), vmem],
        out_shape=[
            jax.ShapeDtypeStruct((SPARE, width, rows), jnp.float32),
            jax.ShapeDtypeStruct((owners, codes // owners + SLAB, width), jnp.float32),
        ],
        scratch_shapes=[
            pltpu.SMEM((rows,), jnp.int32),
            pltpu.VMEM((2 * pieces * owned, width), jnp.float32),
            pltpu.VMEM((block, width), jnp.float32),
            pltpu.VMEM((block, width), jnp.float32),
            pltpu.VMEM((width, codes), jnp.float32),
            pltpu.VMEM((LANES, LANES), jnp.float32),
            pltpu.VMEM((width, rows), jnp.float32),
            pltpu.SemaphoreType.DMA(()),
            pltpu.SemaphoreType.DMA((rows // block,)),
        ],
        compiler_params=pltpu.CompilerParams(vmem_limit_bytes=VLIM),
        name="residuals",
    )(core, ids, codes_t, x, own, other)


def book_bands(book_t, pair):
    half = book_t.shape[1] // 2
    bands = []
    for s in range(2):
        f = slice((2 * pair + s) * SUB_DIM, (2 * pair + s + 1) * SUB_DIM)
        for h in range(2):
            words = book_t[f, h * half : (h + 1) * half]
            hi = words.astype(jnp.bfloat16)
            lo = (words - hi.astype(jnp.float32)).astype(jnp.bfloat16)
            none = jnp.zeros_like(hi)
            bands += [jnp.concatenate([p, none] if s == 0 else [none, p], 1) for p in (hi, lo)]
    return jnp.concatenate(bands, 0)


def errors_kernel(book_ref, codes_ref, rest_hbm, out_ref, table, bands, rest_ref, sems):
    subs, rows = codes_ref.shape
    half = book_ref.shape[0] // 2
    nchunk = sems.shape[0]
    chunk = rows // nchunk
    by_product = bands.shape[0]
    looked_up = subs - 2 * by_product

    def load(c):
        here = pl.ds(c * chunk, chunk)
        return pltpu.make_async_copy(rest_hbm.at[0, :, here], rest_ref.at[:, here], sems.at[c])

    load(0).start()
    load(1).start()
    table[...] = book_ref[...].T
    for q in range(by_product):
        bands[q] = book_bands(table[...], looked_up // 2 + q)
    label = lax.broadcasted_iota(jnp.int32, (half, EBLOCK), 0)

    def product(here):
        acc = jnp.zeros((8, EBLOCK), jnp.float32)
        for q in range(by_product):
            m0 = looked_up + 2 * q
            code = [codes_ref[m : m + 1, here] for m in (m0, m0 + 1)]
            hot = [((c & (half - 1)) == label).astype(jnp.bfloat16) for c in code]
            part = jnp.dot(bands[q], jnp.concatenate(hot, 0), preferred_element_type=jnp.float32)
            for s in range(2):
                p = [part[(4 * s + b) * SUB_DIM : (4 * s + b + 1) * SUB_DIM, :] for b in range(4)]
                word = jnp.where(jnp.broadcast_to(code[s] < half, p[0].shape), p[0] + p[1], p[2] + p[3])
                d = rest_ref[(m0 + s) * SUB_DIM : (m0 + s + 1) * SUB_DIM, here] - word
                d = d * d
                for g in range(0, SUB_DIM, 8):
                    acc = acc + d[g : g + 8, :]
        return acc

    def lookup(cols):
        acc = jnp.zeros((8, LANES), jnp.float32)
        for m in range(looked_up):
            idx = jnp.broadcast_to(codes_ref[m : m + 1, cols], (8, LANES))
            low = idx & (half - 1)
            first = idx < half
            for g in range(0, SUB_DIM, 8):
                f = slice(m * SUB_DIM + g, m * SUB_DIM + g + 8)
                a = jnp.take_along_axis(table[f, 0:half], low, axis=1)
                b = jnp.take_along_axis(table[f, half : 2 * half], low, axis=1)
                d = rest_ref[f, cols] - jnp.where(first, a, b)
                acc = acc + d * d
        return acc

    for c in range(nchunk):
        load(c).wait()
        if c + 2 < nchunk:
            load(c + 2).start()
        for b in range(c * chunk, (c + 1) * chunk, EBLOCK):
            wide = product(slice(b, b + EBLOCK))
            for t in range(0, EBLOCK, LANES):
                acc = wide[:, t : t + LANES] + lookup(slice(b + t, b + t + LANES))
                row = jnp.sum(acc, axis=0, keepdims=True)
                at = (b + t) // LANES
                for k in range(out_ref.shape[0]):
                    out_ref[k, at : at + 1, :] = row


def errors(book, codes_t, rest, copies):
    _, width, rows = rest.shape
    codes = book.shape[0]
    vmem = pl.BlockSpec(memory_space=pltpu.VMEM)
    return pl.pallas_call(
        errors_kernel,
        in_specs=[vmem, vmem, pl.BlockSpec(memory_space=pl.ANY)],
        out_specs=vmem,
        out_shape=jax.ShapeDtypeStruct((copies, rows // LANES, LANES), jnp.float32),
        scratch_shapes=[
            pltpu.VMEM((width, codes), jnp.float32),
            pltpu.VMEM((EPAIRS, LANES, codes), jnp.bfloat16),
            pltpu.VMEM((width, rows), jnp.float32),
            pltpu.SemaphoreType.DMA((4,)),
        ],
        compiler_params=pltpu.CompilerParams(vmem_limit_bytes=40 * 2**20),
        name="errors",
    )(book, codes_t, rest)


def book_kernel(prior, part_ref, old_ref, book_ref, copies_ref):
    total = part_ref[0]
    for k in range(1, part_ref.shape[0]):
        total = total + part_ref[k]
    shape = old_ref.shape
    row = jnp.broadcast_to(total[shape[0] : shape[0] + 1, :], shape)
    lane = lax.broadcasted_iota(jnp.int32, shape, 1)
    code = lax.broadcasted_iota(jnp.int32, shape, 0)
    picked = jnp.where(lane % SUB_DIM == code, row, 0.0)
    r = lax.broadcasted_iota(jnp.int32, (LANES, LANES), 0) // SUB_DIM
    c = lax.broadcasted_iota(jnp.int32, (LANES, LANES), 1) // SUB_DIM
    ones = (r == c).astype(jnp.float32)
    counts = jnp.dot(picked, ones, precision=HIGH, preferred_element_type=jnp.float32)
    book = (total[: shape[0], :] + prior * old_ref[...]) / (counts + prior)
    book_ref[...] = book
    for k in range(copies_ref.shape[0]):
        copies_ref[k] = book


def new_codebook(parts, old, prior):
    return pl.pallas_call(
        functools.partial(book_kernel, prior),
        out_shape=[
            jax.ShapeDtypeStruct(old.shape, jnp.float32),
            jax.ShapeDtypeStruct((parts.shape[0],) + old.shape, jnp.float32),
        ],
        compiler_params=pltpu.CompilerParams(vmem_limit_bytes=4 * 2**20),
        name="codebook",
    )(parts, old)


def swap(x, axis, n, bit):
    return lax.ppermute(x, axis, [(i, i ^ bit) for i in range(n)])


def local(passages, list_ids, code_ids, old_centroids, old_codebook):
    rows, width = passages.shape
    n_row = lax.axis_size("row")
    n_col = lax.axis_size("col")
    total = rows * n_row
    owned_lists = old_centroids.shape[0]
    owned_codes = old_codebook.shape[0]
    lists = owned_lists * n_row
    codes = owned_codes * n_row
    list_prior = float(total // lists)
    code_prior = float(total // codes)
    pieces = n_row // 2
    same_core = [[2 * k + c for k in range(pieces)] for c in range(2)]
    core = (lax.axis_index("row") % 2).astype(jnp.int32).reshape(1)
    codes_t = code_ids.T

    keep, send = list_sums(core, list_ids, passages, pieces, lists)
    pair = keep + swap(send, "row", n_row, 1)
    parts = lax.all_to_all(pair, "row", 0, 0, axis_index_groups=same_core, tiled=True)
    centroids, copies = new_centroids(parts, old_centroids, list_prior)
    own = lax.all_to_all(copies, "row", 0, 0, axis_index_groups=same_core, tiled=True)
    other = swap(own, "row", n_row, 1)
    rest, sums = residuals(core, list_ids, codes_t, passages, own, other, n_row, codes)
    parts = lax.all_to_all(sums, "row", 0, 0, tiled=True)
    codebook, copies = new_codebook(parts, old_codebook, code_prior)
    book = lax.all_to_all(copies, "row", 0, 0, tiled=True).reshape(codes, width)
    err = errors(book, codes_t, rest, n_col)
    err = lax.all_to_all(err, "col", 0, 0, tiled=True)
    return centroids, codebook, jnp.sum(err, axis=0).reshape(rows) / D


def solution(mesh):
    in_specs = (P("row", "col"), P("row"), P("row", "col"), P("row", "col"), P("row", "col"))
    out_specs = (P("row", "col"), P("row", "col"), P("row"))
    return jax.shard_map(local, mesh=mesh, in_specs=in_specs, out_specs=out_specs, check_vma=False)
```

```python
import functools
import jax
import jax.numpy as jnp
from jax import lax
from jax.experimental import pallas as pl
from jax.experimental.pallas import tpu as pltpu

from jax.sharding import PartitionSpec as P

HIGH = lax.Precision.HIGHEST
D = 1024
LANES = 128
SUB_DIM = 16
NACC = 8
SLAB = 8
K1LIM = 50 * 2**20
RBLOCK = 1024
EBLOCK = 512
EPAIRS = 2
VLIM = 24 * 2**20


def sums_kernel(core_ref, ids_hbm, idv_hbm, x_hbm, keep_ref, send_ref, ids, idv, x_ref, lcnt, sems, *accs):
    rows, _ = x_ref.shape
    lists = accs[0].shape[0]
    pieces = keep_ref.shape[0]
    owned = lists // (2 * pieces)
    nchunk = sems.shape[0] - 2
    chunk = rows // nchunk

    def part(c):
        here = pl.ds(c * chunk, chunk)
        return pltpu.make_async_copy(x_hbm.at[here, :], x_ref.at[here, :], sems.at[c])

    fetch_ids = pltpu.make_async_copy(ids_hbm, ids, sems.at[nchunk])
    fetch_idv = pltpu.make_async_copy(idv_hbm, idv, sems.at[nchunk + 1])
    fetch_idv.start()
    fetch_ids.start()
    part(0).start()
    for c in range(1, nchunk):
        part(c).start()

    nhi = lists // LANES
    nt = (((1,), (1,)), ((), ()))

    def counts():
        hi_iota = lax.broadcasted_iota(jnp.int32, (nhi, LANES), 0)
        lo_iota = lax.broadcasted_iota(jnp.int32, (LANES, LANES), 0)
        his, los = [], []
        for t in range(rows // LANES):
            row = idv[t : t + 1, :]
            his.append((lax.shift_right_logical(row, 7) == hi_iota).astype(jnp.bfloat16))
            los.append(((row & (LANES - 1)) == lo_iota).astype(jnp.bfloat16))
        lcnt[...] = lax.dot_general(
            jnp.concatenate(his, 1), jnp.concatenate(los, 1), nt, preferred_element_type=jnp.float32
        )

    def scatter(start):
        for u in range(0, CBLOCK, NACC):
            row = [ids.at[pl.ds(u + j, rows - CBLOCK + 1)][start] for j in range(NACC)]
            old = [accs[j][pl.ds(row[j], 1), :] for j in range(NACC)]
            new = [x_ref[pl.ds(start + u + j, 1), :] for j in range(NACC)]
            for j in range(NACC):
                accs[j][pl.ds(row[j], 1), :] = old[j] + new[j]

    for acc in accs[: NACC // 2]:
        acc[...] = jnp.zeros_like(acc)
    fetch_idv.wait()
    for acc in accs[NACC // 2 :]:
        acc[...] = jnp.zeros_like(acc)
    counts()
    fetch_ids.wait()

    @pl.loop(0, nchunk)
    def _(c):
        part(c).wait()

        @pl.loop(0, chunk // CBLOCK)
        def _(i):
            start = pl.multiple_of(c * chunk + i * CBLOCK, CBLOCK)
            scatter(start)

    core = core_ref[0]
    for out, par in ((send_ref, 1 - core), (keep_ref, core)):
        @pl.loop(0, pieces)
        def _(k):
            owner = 2 * k + par
            start = pl.multiple_of(owner * owned, owned)
            total = accs[0][pl.ds(start, owned), :]
            for acc in accs[1:]:
                total = total + acc[pl.ds(start, owned), :]
            out[k, 0:owned, :] = total
            out[k, pl.ds(owned, SLAB), :] = jnp.concatenate(
                [
                    lcnt[pl.ds(owner * (owned // LANES), owned // LANES), :],
                    jnp.zeros((SLAB - owned // LANES, LANES), jnp.float32),
                ],
                0,
            )


CBLOCK = 1024
NCHUNK = 8


def list_sums(core, ids, x, pieces, lists):
    rows, width = x.shape
    idv = ids.reshape(rows // LANES, LANES)
    ids = pltpu.with_memory_space_constraint(ids, pltpu.HBM)
    idv = pltpu.with_memory_space_constraint(idv, pltpu.HBM)
    owned = lists // (2 * pieces)
    out = jax.ShapeDtypeStruct((pieces, owned + SLAB, width), jnp.float32)
    hbm = pl.BlockSpec(memory_space=pltpu.HBM)
    vmem = pl.BlockSpec(memory_space=pltpu.VMEM)
    return pl.pallas_call(
        sums_kernel,
        in_specs=[pl.BlockSpec(memory_space=pltpu.SMEM)] + [hbm] * 3,
        out_specs=[vmem, vmem],
        out_shape=[out, out],
        scratch_shapes=[
            pltpu.SMEM((rows,), jnp.int32),
            pltpu.VMEM((rows // LANES, LANES), jnp.int32),
            pltpu.VMEM((rows, width), jnp.float32),
            pltpu.VMEM((lists // LANES, LANES), jnp.float32),
            pltpu.SemaphoreType.DMA((NCHUNK + 2,)),
        ]
        + [pltpu.VMEM((lists, width), jnp.float32)] * NACC,
        compiler_params=pltpu.CompilerParams(vmem_limit_bytes=K1LIM),
        name="list_sums",
    )(core, ids, idv, x)


def centroid_kernel(prior, part_ref, old_ref, cent_ref, copies_ref):
    owned = old_ref.shape[0]
    total = part_ref[0]
    for k in range(1, part_ref.shape[0]):
        total = total + part_ref[k]
    eye = (
        lax.broadcasted_iota(jnp.int32, (LANES, LANES), 0)
        == lax.broadcasted_iota(jnp.int32, (LANES, LANES), 1)
    )
    for h in range(owned // LANES):
        row = total[owned + h : owned + h + 1, :]
        col = jnp.sum(jnp.where(eye, row, 0.0), axis=1, keepdims=True)
        sl = slice(h * LANES, (h + 1) * LANES)
        cent = (total[sl, :] + prior * old_ref[sl, :]) / (col + prior)
        cent_ref[sl, :] = cent
        for k in range(copies_ref.shape[0]):
            copies_ref[k, sl, :] = cent


def new_centroids(parts, old, prior):
    n = parts.shape[0]
    return pl.pallas_call(
        functools.partial(centroid_kernel, prior),
        out_shape=[
            jax.ShapeDtypeStruct(old.shape, jnp.float32),
            jax.ShapeDtypeStruct((n,) + old.shape, jnp.float32),
        ],
        compiler_params=pltpu.CompilerParams(vmem_limit_bytes=16 * 2**20),
        name="centroids",
    )(parts, old)


NT = (((1,), (1,)), ((), ()))


def resid_kernel(
    core_ref, ids_ref, codes_ref, x_ref, own_ref, other_ref, rest_ref, sums_ref, ids, table, got0, got1, sumst, ccnt, sems
):
    block = got0.shape[0]
    rows = x_ref.shape[0]
    pieces, owned, _ = own_ref.shape
    subs = codes_ref.shape[0]
    owners, slab, _ = sums_ref.shape
    each = slab - SLAB
    half = owners * each // 2
    early, late = pl.ds(0, 2 * block), pl.ds(2 * block, rows - 2 * block)
    fetch = [pltpu.make_async_copy(ids_ref.at[p], ids.at[p], sems.at[n]) for n, p in enumerate((early, late))]
    for f in fetch:
        f.start()
    core = core_ref[0]
    for k in range(pieces):
        table[pl.ds(pl.multiple_of((2 * k + core) * owned, owned), owned), :] = own_ref[k]
        table[pl.ds(pl.multiple_of((2 * k + 1 - core) * owned, owned), owned), :] = other_ref[k]
    sumst[...] = jnp.zeros_like(sumst)
    ccnt[...] = jnp.zeros_like(ccnt)
    fetch[0].wait()

    sublane = lax.broadcasted_iota(jnp.int32, (8, LANES), 0)

    def gather(start, got):
        for g in range(0, block, 8):
            tile = None
            for j in range(8):
                row = ids.at[pl.ds(g + j, rows - block + 1)][start]
                line = jnp.broadcast_to(table[pl.ds(row, 1), :], (8, LANES))
                tile = line if j == 0 else jnp.where(sublane == j, line, tile)
            got[g : g + 8, :] = tile

    def work(start, got):
        here = pl.ds(start, block)
        rest = (x_ref[here, :] - got[...]).T
        rest_ref[:, here] = rest
        hi = rest.astype(jnp.bfloat16)
        lo = (rest - hi.astype(jnp.float32)).astype(jnp.bfloat16)
        label = lax.broadcasted_iota(jnp.int32, (half, block), 0)
        digit = lax.broadcasted_iota(jnp.int32, (SUB_DIM, block), 0)
        left, right = [], []
        for m in range(subs):
            code = codes_ref[pl.ds(m, 1), here]
            left.append((lax.shift_right_logical(code, 4) == digit).astype(jnp.bfloat16))
            right.append(((code & (SUB_DIM - 1)) == digit).astype(jnp.bfloat16))
        ccnt[...] += lax.dot_general(
            jnp.concatenate(left, 0), jnp.concatenate(right, 0), NT, preferred_element_type=jnp.float32
        )
        for p in range(subs // 2):
            left, right = [], []
            for m in (2 * p, 2 * p + 1):
                code = codes_ref[pl.ds(m, 1), here]
                right.append(((code & (half - 1)) == label).astype(jnp.bfloat16))
                f = slice(m * SUB_DIM, (m + 1) * SUB_DIM)
                both = jnp.concatenate([hi[f], lo[f]], 0)
                top = jnp.broadcast_to((code < half).astype(jnp.bfloat16), both.shape)
                first = both * top
                left += [first, both - first]
            part = lax.dot_general(
                jnp.concatenate(left, 0), jnp.concatenate(right, 0), NT, preferred_element_type=jnp.float32
            )
            for s in range(2):
                f = slice((2 * p + s) * SUB_DIM, (2 * p + s + 1) * SUB_DIM)
                for h in range(2):
                    band = part[(4 * s + 2 * h) * SUB_DIM : (4 * s + 2 * h + 2) * SUB_DIM, s * half : (s + 1) * half]
                    sumst[f, h * half : (h + 1) * half] += band[:SUB_DIM] + band[SUB_DIM:]

    gather(0, got0)
    fetch[1].wait()

    @pl.loop(0, rows // (2 * block))
    def _(i):
        first = pl.multiple_of(2 * i * block, block)
        second = pl.multiple_of(first + block, block)
        third = pl.multiple_of(jnp.minimum(second + block, rows - block), block)
        gather(second, got1)
        work(first, got0)
        gather(third, got0)
        work(second, got1)

    total = sumst[...].T
    cc = ccnt[...]
    r = lax.broadcasted_iota(jnp.int32, cc.shape, 0) // SUB_DIM
    c = lax.broadcasted_iota(jnp.int32, cc.shape, 1) // SUB_DIM
    cc = jnp.where(r == c, cc, 0.0)
    crow = cc[0:SUB_DIM, :]
    for m in range(1, subs):
        crow = crow + cc[m * SUB_DIM : (m + 1) * SUB_DIM, :]
    fill = jnp.zeros((SLAB - 1, LANES), jnp.float32)
    for o in range(owners):
        sums_ref[o, 0:each, :] = total[o * each : (o + 1) * each, :]
        sums_ref[o, each:slab, :] = jnp.concatenate([crow[o : o + 1, :], fill], 0)


def residuals(core, ids, codes_t, x, own, other, owners, codes, block=RBLOCK):
    rows, width = x.shape
    pieces, owned, _ = own.shape
    vmem = pl.BlockSpec(memory_space=pltpu.VMEM)
    return pl.pallas_call(
        resid_kernel,
        in_specs=[pl.BlockSpec(memory_space=pltpu.SMEM)] + [vmem] * 5,
        out_specs=[vmem, vmem],
        out_shape=[
            jax.ShapeDtypeStruct((width, rows), jnp.float32),
            jax.ShapeDtypeStruct((owners, codes // owners + SLAB, width), jnp.float32),
        ],
        scratch_shapes=[
            pltpu.SMEM((rows,), jnp.int32),
            pltpu.VMEM((2 * pieces * owned, width), jnp.float32),
            pltpu.VMEM((block, width), jnp.float32),
            pltpu.VMEM((block, width), jnp.float32),
            pltpu.VMEM((width, codes), jnp.float32),
            pltpu.VMEM((LANES, LANES), jnp.float32),
            pltpu.SemaphoreType.DMA((2,)),
        ],
        compiler_params=pltpu.CompilerParams(vmem_limit_bytes=VLIM),
        name="residuals",
    )(core, ids, codes_t, x, own, other)


def book_bands(book_t, pair):
    half = book_t.shape[1] // 2
    bands = []
    for s in range(2):
        f = slice((2 * pair + s) * SUB_DIM, (2 * pair + s + 1) * SUB_DIM)
        for h in range(2):
            words = book_t[f, h * half : (h + 1) * half]
            hi = words.astype(jnp.bfloat16)
            lo = (words - hi.astype(jnp.float32)).astype(jnp.bfloat16)
            none = jnp.zeros_like(hi)
            bands += [jnp.concatenate([p, none] if s == 0 else [none, p], 1) for p in (hi, lo)]
    return jnp.concatenate(bands, 0)


def errors_kernel(book_ref, codes_ref, rest_ref, out_ref, table, bands):
    subs, rows = codes_ref.shape
    half = book_ref.shape[0] // 2
    by_product = bands.shape[0]
    looked_up = subs - 2 * by_product

    table[...] = book_ref[...].T
    for q in range(by_product):
        bands[q] = book_bands(table[...], looked_up // 2 + q)
    label = lax.broadcasted_iota(jnp.int32, (half, EBLOCK), 0)

    def product(here):
        acc = jnp.zeros((8, EBLOCK), jnp.float32)
        for q in range(by_product):
            m0 = looked_up + 2 * q
            code = [codes_ref[m : m + 1, here] for m in (m0, m0 + 1)]
            hot = [((c & (half - 1)) == label).astype(jnp.bfloat16) for c in code]
            part = jnp.dot(bands[q], jnp.concatenate(hot, 0), preferred_element_type=jnp.float32)
            for s in range(2):
                p = [part[(4 * s + b) * SUB_DIM : (4 * s + b + 1) * SUB_DIM, :] for b in range(4)]
                word = jnp.where(jnp.broadcast_to(code[s] < half, p[0].shape), p[0] + p[1], p[2] + p[3])
                d = rest_ref[(m0 + s) * SUB_DIM : (m0 + s + 1) * SUB_DIM, here] - word
                d = d * d
                for g in range(0, SUB_DIM, 8):
                    acc = acc + d[g : g + 8, :]
        return acc

    def lookup(cols):
        acc = jnp.zeros((8, LANES), jnp.float32)
        for m in range(looked_up):
            idx = jnp.broadcast_to(codes_ref[m : m + 1, cols], (8, LANES))
            low = idx & (half - 1)
            first = idx < half
            for g in range(0, SUB_DIM, 8):
                f = slice(m * SUB_DIM + g, m * SUB_DIM + g + 8)
                a = jnp.take_along_axis(table[f, 0:half], low, axis=1)
                b = jnp.take_along_axis(table[f, half : 2 * half], low, axis=1)
                d = rest_ref[f, cols] - jnp.where(first, a, b)
                acc = acc + d * d
        return acc

    for b in range(0, rows, EBLOCK):
        wide = product(slice(b, b + EBLOCK))
        for t in range(0, EBLOCK, LANES):
            acc = wide[:, t : t + LANES] + lookup(slice(b + t, b + t + LANES))
            row = jnp.sum(acc, axis=0, keepdims=True)
            at = (b + t) // LANES
            for k in range(out_ref.shape[0]):
                out_ref[k, at : at + 1, :] = row


def errors(book, codes_t, rest, copies):
    width, rows = rest.shape
    codes = book.shape[0]
    vmem = pl.BlockSpec(memory_space=pltpu.VMEM)
    return pl.pallas_call(
        errors_kernel,
        in_specs=[vmem] * 3,
        out_specs=vmem,
        out_shape=jax.ShapeDtypeStruct((copies, rows // LANES, LANES), jnp.float32),
        scratch_shapes=[
            pltpu.VMEM((width, codes), jnp.float32),
            pltpu.VMEM((EPAIRS, LANES, codes), jnp.bfloat16),
        ],
        compiler_params=pltpu.CompilerParams(vmem_limit_bytes=24 * 2**20),
        name="errors",
    )(book, codes_t, rest)


def book_kernel(prior, part_ref, old_ref, book_ref, copies_ref):
    total = part_ref[0]
    for k in range(1, part_ref.shape[0]):
        total = total + part_ref[k]
    shape = old_ref.shape
    row = jnp.broadcast_to(total[shape[0] : shape[0] + 1, :], shape)
    lane = lax.broadcasted_iota(jnp.int32, shape, 1)
    code = lax.broadcasted_iota(jnp.int32, shape, 0)
    picked = jnp.where(lane % SUB_DIM == code, row, 0.0)
    r = lax.broadcasted_iota(jnp.int32, (LANES, LANES), 0) // SUB_DIM
    c = lax.broadcasted_iota(jnp.int32, (LANES, LANES), 1) // SUB_DIM
    ones = (r == c).astype(jnp.float32)
    counts = jnp.dot(picked, ones, precision=HIGH, preferred_element_type=jnp.float32)
    book = (total[: shape[0], :] + prior * old_ref[...]) / (counts + prior)
    book_ref[...] = book
    for k in range(copies_ref.shape[0]):
        copies_ref[k] = book


def new_codebook(parts, old, prior):
    return pl.pallas_call(
        functools.partial(book_kernel, prior),
        out_shape=[
            jax.ShapeDtypeStruct(old.shape, jnp.float32),
            jax.ShapeDtypeStruct((parts.shape[0],) + old.shape, jnp.float32),
        ],
        compiler_params=pltpu.CompilerParams(vmem_limit_bytes=4 * 2**20),
        name="codebook",
    )(parts, old)


def swap(x, axis, n, bit):
    return lax.ppermute(x, axis, [(i, i ^ bit) for i in range(n)])


def local(passages, list_ids, code_ids, old_centroids, old_codebook):
    rows, width = passages.shape
    n_row = lax.axis_size("row")
    n_col = lax.axis_size("col")
    total = rows * n_row
    owned_lists = old_centroids.shape[0]
    owned_codes = old_codebook.shape[0]
    lists = owned_lists * n_row
    codes = owned_codes * n_row
    list_prior = float(total // lists)
    code_prior = float(total // codes)
    pieces = n_row // 2
    same_core = [[2 * k + c for k in range(pieces)] for c in range(2)]
    core = (lax.axis_index("row") % 2).astype(jnp.int32).reshape(1)
    codes_t = code_ids.T

    keep, send = list_sums(core, list_ids, passages, pieces, lists)
    pair = keep + swap(send, "row", n_row, 1)
    parts = lax.all_to_all(pair, "row", 0, 0, axis_index_groups=same_core, tiled=True)
    centroids, copies = new_centroids(parts, old_centroids, list_prior)
    own = lax.all_to_all(copies, "row", 0, 0, axis_index_groups=same_core, tiled=True)
    other = swap(own, "row", n_row, 1)
    rest, sums = residuals(core, list_ids, codes_t, passages, own, other, n_row, codes)
    parts = lax.all_to_all(sums, "row", 0, 0, tiled=True)
    codebook, copies = new_codebook(parts, old_codebook, code_prior)
    book = lax.all_to_all(copies, "row", 0, 0, tiled=True).reshape(codes, width)
    err = errors(book, codes_t, rest, n_col)
    err = lax.all_to_all(err, "col", 0, 0, tiled=True)
    return centroids, codebook, jnp.sum(err, axis=0).reshape(rows) / D


def solution(mesh):
    in_specs = (P("row", "col"), P("row"), P("row", "col"), P("row", "col"), P("row", "col"))
    out_specs = (P("row", "col"), P("row", "col"), P("row"))
    return jax.shard_map(local, mesh=mesh, in_specs=in_specs, out_specs=out_specs, check_vma=False)
```

```python
import functools
import jax
import jax.numpy as jnp
from jax import lax
from jax.experimental import pallas as pl
from jax.experimental.pallas import tpu as pltpu

from jax.sharding import PartitionSpec as P

HIGH = lax.Precision.HIGHEST
D = 1024
LANES = 128
SUB_DIM = 16
NACC = 8
SLAB = 8
K1LIM = 50 * 2**20
RBLOCK = 256
UNROLL = 8
EBLOCK = 512
EPAIRS = 2
VLIM = 24 * 2**20


def sums_kernel(core_ref, ids_hbm, idv_hbm, x_hbm, keep_ref, send_ref, ids, idv, x_ref, lcnt, sems, *accs):
    rows, _ = x_ref.shape
    lists = accs[0].shape[0]
    pieces = keep_ref.shape[0]
    owned = lists // (2 * pieces)
    nchunk = sems.shape[0] - 2
    chunk = rows // nchunk

    def part(c):
        here = pl.ds(c * chunk, chunk)
        return pltpu.make_async_copy(x_hbm.at[here, :], x_ref.at[here, :], sems.at[c])

    fetch_ids = pltpu.make_async_copy(ids_hbm, ids, sems.at[nchunk])
    fetch_idv = pltpu.make_async_copy(idv_hbm, idv, sems.at[nchunk + 1])
    fetch_idv.start()
    fetch_ids.start()
    part(0).start()
    for c in range(1, nchunk):
        part(c).start()

    nhi = lists // LANES
    nt = (((1,), (1,)), ((), ()))

    def counts():
        hi_iota = lax.broadcasted_iota(jnp.int32, (nhi, LANES), 0)
        lo_iota = lax.broadcasted_iota(jnp.int32, (LANES, LANES), 0)
        his, los = [], []
        for t in range(rows // LANES):
            row = idv[t : t + 1, :]
            his.append((lax.shift_right_logical(row, 7) == hi_iota).astype(jnp.bfloat16))
            los.append(((row & (LANES - 1)) == lo_iota).astype(jnp.bfloat16))
        lcnt[...] = lax.dot_general(
            jnp.concatenate(his, 1), jnp.concatenate(los, 1), nt, preferred_element_type=jnp.float32
        )

    def scatter(start):
        for u in range(0, CBLOCK, NACC):
            row = [ids.at[pl.ds(u + j, rows - CBLOCK + 1)][start] for j in range(NACC)]
            old = [accs[j][pl.ds(row[j], 1), :] for j in range(NACC)]
            new = [x_ref[pl.ds(start + u + j, 1), :] for j in range(NACC)]
            for j in range(NACC):
                accs[j][pl.ds(row[j], 1), :] = old[j] + new[j]

    for acc in accs[: NACC // 2]:
        acc[...] = jnp.zeros_like(acc)
    fetch_idv.wait()
    for acc in accs[NACC // 2 :]:
        acc[...] = jnp.zeros_like(acc)
    counts()
    fetch_ids.wait()

    @pl.loop(0, nchunk)
    def _(c):
        part(c).wait()

        @pl.loop(0, chunk // CBLOCK)
        def _(i):
            start = pl.multiple_of(c * chunk + i * CBLOCK, CBLOCK)
            scatter(start)

    core = core_ref[0]
    for out, par in ((send_ref, 1 - core), (keep_ref, core)):
        @pl.loop(0, pieces)
        def _(k):
            owner = 2 * k + par
            start = pl.multiple_of(owner * owned, owned)
            total = accs[0][pl.ds(start, owned), :]
            for acc in accs[1:]:
                total = total + acc[pl.ds(start, owned), :]
            out[k, 0:owned, :] = total
            out[k, pl.ds(owned, SLAB), :] = jnp.concatenate(
                [
                    lcnt[pl.ds(owner * (owned // LANES), owned // LANES), :],
                    jnp.zeros((SLAB - owned // LANES, LANES), jnp.float32),
                ],
                0,
            )


CBLOCK = 1024
NCHUNK = 8


def list_sums(core, ids, x, pieces, lists):
    rows, width = x.shape
    idv = ids.reshape(rows // LANES, LANES)
    ids = pltpu.with_memory_space_constraint(ids, pltpu.HBM)
    idv = pltpu.with_memory_space_constraint(idv, pltpu.HBM)
    owned = lists // (2 * pieces)
    out = jax.ShapeDtypeStruct((pieces, owned + SLAB, width), jnp.float32)
    hbm = pl.BlockSpec(memory_space=pltpu.HBM)
    vmem = pl.BlockSpec(memory_space=pltpu.VMEM)
    return pl.pallas_call(
        sums_kernel,
        in_specs=[pl.BlockSpec(memory_space=pltpu.SMEM)] + [hbm] * 3,
        out_specs=[vmem, vmem],
        out_shape=[out, out],
        scratch_shapes=[
            pltpu.SMEM((rows,), jnp.int32),
            pltpu.VMEM((rows // LANES, LANES), jnp.int32),
            pltpu.VMEM((rows, width), jnp.float32),
            pltpu.VMEM((lists // LANES, LANES), jnp.float32),
            pltpu.SemaphoreType.DMA((NCHUNK + 2,)),
        ]
        + [pltpu.VMEM((lists, width), jnp.float32)] * NACC,
        compiler_params=pltpu.CompilerParams(vmem_limit_bytes=K1LIM),
        name="list_sums",
    )(core, ids, idv, x)


def code_counts_kernel(codes_ref, out_ref):
    subs, rows = codes_ref.shape
    digit = lax.broadcasted_iota(jnp.int32, (SUB_DIM, CBLOCK), 0)
    cc = jnp.zeros((LANES, LANES), jnp.float32)
    for b in range(0, rows, CBLOCK):
        left, right = [], []
        for m in range(subs):
            code = codes_ref[m : m + 1, b : b + CBLOCK]
            left.append((lax.shift_right_logical(code, 4) == digit).astype(jnp.bfloat16))
            right.append(((code & (SUB_DIM - 1)) == digit).astype(jnp.bfloat16))
        cc += lax.dot_general(
            jnp.concatenate(left, 0), jnp.concatenate(right, 0), NT, preferred_element_type=jnp.float32
        )
    r = lax.broadcasted_iota(jnp.int32, cc.shape, 0) // SUB_DIM
    c = lax.broadcasted_iota(jnp.int32, cc.shape, 1) // SUB_DIM
    cc = jnp.where(r == c, cc, 0.0)
    total = cc[0:SUB_DIM, :]
    for m in range(1, subs):
        total = total + cc[m * SUB_DIM : (m + 1) * SUB_DIM, :]
    out_ref[...] = total


def code_counts(codes_t):
    vmem = pl.BlockSpec(memory_space=pltpu.VMEM)
    return pl.pallas_call(
        code_counts_kernel,
        in_specs=[vmem],
        out_specs=vmem,
        out_shape=jax.ShapeDtypeStruct((SUB_DIM, LANES), jnp.float32),
        compiler_params=pltpu.CompilerParams(vmem_limit_bytes=8 * 2**20),
        cost_estimate=pl.CostEstimate(flops=10**9, bytes_accessed=4 * 10**6, transcendentals=0),
        name="code_counts",
    )(codes_t)


def centroid_kernel(prior, part_ref, old_ref, cent_ref, copies_ref):
    owned = old_ref.shape[0]
    total = part_ref[0]
    for k in range(1, part_ref.shape[0]):
        total = total + part_ref[k]
    eye = (
        lax.broadcasted_iota(jnp.int32, (LANES, LANES), 0)
        == lax.broadcasted_iota(jnp.int32, (LANES, LANES), 1)
    )
    for h in range(owned // LANES):
        row = total[owned + h : owned + h + 1, :]
        col = jnp.sum(jnp.where(eye, row, 0.0), axis=1, keepdims=True)
        sl = slice(h * LANES, (h + 1) * LANES)
        cent = (total[sl, :] + prior * old_ref[sl, :]) / (col + prior)
        cent_ref[sl, :] = cent
        for k in range(copies_ref.shape[0]):
            copies_ref[k, sl, :] = cent


def new_centroids(parts, old, prior):
    n = parts.shape[0]
    return pl.pallas_call(
        functools.partial(centroid_kernel, prior),
        out_shape=[
            jax.ShapeDtypeStruct(old.shape, jnp.float32),
            jax.ShapeDtypeStruct((n,) + old.shape, jnp.float32),
        ],
        compiler_params=pltpu.CompilerParams(vmem_limit_bytes=16 * 2**20),
        name="centroids",
    )(parts, old)


NT = (((1,), (1,)), ((), ()))


def resid_kernel(
    core_ref, ids_ref, codes_ref, x_ref, own_ref, other_ref, counts_ref, rest_ref, sums_ref, ids, table, got0, got1, sumst, sems
):
    block = got0.shape[0]
    rows = x_ref.shape[0]
    pieces, owned, _ = own_ref.shape
    subs = codes_ref.shape[0]
    owners, slab, _ = sums_ref.shape
    each = slab - SLAB
    half = owners * each // 2
    early, late = pl.ds(0, 2 * block), pl.ds(2 * block, rows - 2 * block)
    fetch = [pltpu.make_async_copy(ids_ref.at[p], ids.at[p], sems.at[n]) for n, p in enumerate((early, late))]
    for f in fetch:
        f.start()
    core = core_ref[0]
    for k in range(pieces):
        table[pl.ds(pl.multiple_of((2 * k + core) * owned, owned), owned), :] = own_ref[k]
        table[pl.ds(pl.multiple_of((2 * k + 1 - core) * owned, owned), owned), :] = other_ref[k]
    sumst[...] = jnp.zeros_like(sumst)
    fetch[0].wait()

    sublane = lax.broadcasted_iota(jnp.int32, (8, LANES), 0)

    def gather(start, got):
        for g in range(0, block, 8):
            tile = None
            for j in range(8):
                row = ids.at[pl.ds(g + j, rows - block + 1)][start]
                line = jnp.broadcast_to(table[pl.ds(row, 1), :], (8, LANES))
                tile = line if j == 0 else jnp.where(sublane == j, line, tile)
            got[g : g + 8, :] = tile

    def work(start, got):
        here = pl.ds(start, block)
        rest = (x_ref[here, :] - got[...]).T
        rest_ref[:, here] = rest
        hi = rest.astype(jnp.bfloat16)
        lo = (rest - hi.astype(jnp.float32)).astype(jnp.bfloat16)
        label = lax.broadcasted_iota(jnp.int32, (half, block), 0)
        for p in range(subs // 2):
            left, right = [], []
            for m in (2 * p, 2 * p + 1):
                code = codes_ref[pl.ds(m, 1), here]
                right.append(((code & (half - 1)) == label).astype(jnp.bfloat16))
                f = slice(m * SUB_DIM, (m + 1) * SUB_DIM)
                both = jnp.concatenate([hi[f], lo[f]], 0)
                top = jnp.broadcast_to((code < half).astype(jnp.bfloat16), both.shape)
                first = both * top
                left += [first, both - first]
            part = lax.dot_general(
                jnp.concatenate(left, 0), jnp.concatenate(right, 0), NT, preferred_element_type=jnp.float32
            )
            for s in range(2):
                f = slice((2 * p + s) * SUB_DIM, (2 * p + s + 1) * SUB_DIM)
                for h in range(2):
                    band = part[(4 * s + 2 * h) * SUB_DIM : (4 * s + 2 * h + 2) * SUB_DIM, s * half : (s + 1) * half]
                    sumst[f, h * half : (h + 1) * half] += band[:SUB_DIM] + band[SUB_DIM:]

    gather(0, got0)
    fetch[1].wait()

    @pl.loop(0, rows // (UNROLL * block))
    def _(i):
        base = pl.multiple_of(i * UNROLL * block, block)
        for u in range(UNROLL):
            now, after = (got0, got1) if u % 2 == 0 else (got1, got0)
            here = pl.multiple_of(base + u * block, block)
            gather(pl.multiple_of(jnp.minimum(here + block, rows - block), block), after)
            work(here, now)

    total = sumst[...].T
    fill = jnp.zeros((SLAB - 1, LANES), jnp.float32)
    for o in range(owners):
        sums_ref[o, 0:each, :] = total[o * each : (o + 1) * each, :]
        sums_ref[o, each:slab, :] = jnp.concatenate([counts_ref[o : o + 1, :], fill], 0)


def residuals(core, ids, codes_t, x, own, other, counts, owners, codes, block=RBLOCK):
    rows, width = x.shape
    pieces, owned, _ = own.shape
    vmem = pl.BlockSpec(memory_space=pltpu.VMEM)
    return pl.pallas_call(
        resid_kernel,
        in_specs=[pl.BlockSpec(memory_space=pltpu.SMEM)] + [vmem] * 6,
        out_specs=[vmem, vmem],
        out_shape=[
            jax.ShapeDtypeStruct((width, rows), jnp.float32),
            jax.ShapeDtypeStruct((owners, codes // owners + SLAB, width), jnp.float32),
        ],
        scratch_shapes=[
            pltpu.SMEM((rows,), jnp.int32),
            pltpu.VMEM((2 * pieces * owned, width), jnp.float32),
            pltpu.VMEM((block, width), jnp.float32),
            pltpu.VMEM((block, width), jnp.float32),
            pltpu.VMEM((width, codes), jnp.float32),
            pltpu.SemaphoreType.DMA((2,)),
        ],
        compiler_params=pltpu.CompilerParams(vmem_limit_bytes=VLIM),
        name="residuals",
    )(core, ids, codes_t, x, own, other, counts)


def book_bands(book_t, pair):
    half = book_t.shape[1] // 2
    bands = []
    for s in range(2):
        f = slice((2 * pair + s) * SUB_DIM, (2 * pair + s + 1) * SUB_DIM)
        for h in range(2):
            words = book_t[f, h * half : (h + 1) * half]
            hi = words.astype(jnp.bfloat16)
            lo = (words - hi.astype(jnp.float32)).astype(jnp.bfloat16)
            none = jnp.zeros_like(hi)
            bands += [jnp.concatenate([p, none] if s == 0 else [none, p], 1) for p in (hi, lo)]
    return jnp.concatenate(bands, 0)


def errors_kernel(book_ref, codes_ref, rest_ref, out_ref, table, bands):
    subs, rows = codes_ref.shape
    half = book_ref.shape[0] // 2
    by_product = bands.shape[0]
    looked_up = subs - 2 * by_product

    table[...] = book_ref[...].T
    for q in range(by_product):
        bands[q] = book_bands(table[...], looked_up // 2 + q)
    label = lax.broadcasted_iota(jnp.int32, (half, EBLOCK), 0)

    def product(here):
        acc = jnp.zeros((8, EBLOCK), jnp.float32)
        for q in range(by_product):
            m0 = looked_up + 2 * q
            code = [codes_ref[m : m + 1, here] for m in (m0, m0 + 1)]
            hot = [((c & (half - 1)) == label).astype(jnp.bfloat16) for c in code]
            part = jnp.dot(bands[q], jnp.concatenate(hot, 0), preferred_element_type=jnp.float32)
            for s in range(2):
                p = [part[(4 * s + b) * SUB_DIM : (4 * s + b + 1) * SUB_DIM, :] for b in range(4)]
                word = jnp.where(jnp.broadcast_to(code[s] < half, p[0].shape), p[0] + p[1], p[2] + p[3])
                d = rest_ref[(m0 + s) * SUB_DIM : (m0 + s + 1) * SUB_DIM, here] - word
                d = d * d
                for g in range(0, SUB_DIM, 8):
                    acc = acc + d[g : g + 8, :]
        return acc

    def lookup(cols):
        acc = jnp.zeros((8, LANES), jnp.float32)
        for m in range(looked_up):
            idx = jnp.broadcast_to(codes_ref[m : m + 1, cols], (8, LANES))
            low = idx & (half - 1)
            first = idx < half
            for g in range(0, SUB_DIM, 8):
                f = slice(m * SUB_DIM + g, m * SUB_DIM + g + 8)
                a = jnp.take_along_axis(table[f, 0:half], low, axis=1)
                b = jnp.take_along_axis(table[f, half : 2 * half], low, axis=1)
                d = rest_ref[f, cols] - jnp.where(first, a, b)
                acc = acc + d * d
        return acc

    for b in range(0, rows, EBLOCK):
        wide = product(slice(b, b + EBLOCK))
        for t in range(0, EBLOCK, LANES):
            acc = wide[:, t : t + LANES] + lookup(slice(b + t, b + t + LANES))
            row = jnp.sum(acc, axis=0, keepdims=True)
            at = (b + t) // LANES
            for k in range(out_ref.shape[0]):
                out_ref[k, at : at + 1, :] = row


def errors(book, codes_t, rest, copies):
    width, rows = rest.shape
    codes = book.shape[0]
    vmem = pl.BlockSpec(memory_space=pltpu.VMEM)
    return pl.pallas_call(
        errors_kernel,
        in_specs=[vmem] * 3,
        out_specs=vmem,
        out_shape=jax.ShapeDtypeStruct((copies, rows // LANES, LANES), jnp.float32),
        scratch_shapes=[
            pltpu.VMEM((width, codes), jnp.float32),
            pltpu.VMEM((EPAIRS, LANES, codes), jnp.bfloat16),
        ],
        compiler_params=pltpu.CompilerParams(vmem_limit_bytes=24 * 2**20),
        name="errors",
    )(book, codes_t, rest)


def book_kernel(prior, part_ref, old_ref, book_ref, copies_ref):
    total = part_ref[0]
    for k in range(1, part_ref.shape[0]):
        total = total + part_ref[k]
    shape = old_ref.shape
    row = jnp.broadcast_to(total[shape[0] : shape[0] + 1, :], shape)
    lane = lax.broadcasted_iota(jnp.int32, shape, 1)
    code = lax.broadcasted_iota(jnp.int32, shape, 0)
    picked = jnp.where(lane % SUB_DIM == code, row, 0.0)
    r = lax.broadcasted_iota(jnp.int32, (LANES, LANES), 0) // SUB_DIM
    c = lax.broadcasted_iota(jnp.int32, (LANES, LANES), 1) // SUB_DIM
    ones = (r == c).astype(jnp.float32)
    counts = jnp.dot(picked, ones, precision=HIGH, preferred_element_type=jnp.float32)
    book = (total[: shape[0], :] + prior * old_ref[...]) / (counts + prior)
    book_ref[...] = book
    for k in range(copies_ref.shape[0]):
        copies_ref[k] = book


def new_codebook(parts, old, prior):
    return pl.pallas_call(
        functools.partial(book_kernel, prior),
        out_shape=[
            jax.ShapeDtypeStruct(old.shape, jnp.float32),
            jax.ShapeDtypeStruct((parts.shape[0],) + old.shape, jnp.float32),
        ],
        compiler_params=pltpu.CompilerParams(vmem_limit_bytes=4 * 2**20),
        name="codebook",
    )(parts, old)


def swap(x, axis, n, bit):
    return lax.ppermute(x, axis, [(i, i ^ bit) for i in range(n)])


def local(passages, list_ids, code_ids, old_centroids, old_codebook):
    rows, width = passages.shape
    n_row = lax.axis_size("row")
    n_col = lax.axis_size("col")
    total = rows * n_row
    owned_lists = old_centroids.shape[0]
    owned_codes = old_codebook.shape[0]
    lists = owned_lists * n_row
    codes = owned_codes * n_row
    list_prior = float(total // lists)
    code_prior = float(total // codes)
    pieces = n_row // 2
    same_core = [[2 * k + c for k in range(pieces)] for c in range(2)]
    core = (lax.axis_index("row") % 2).astype(jnp.int32).reshape(1)
    codes_t = code_ids.T

    keep, send = list_sums(core, list_ids, passages, pieces, lists)
    pair = keep + swap(send, "row", n_row, 1)
    parts = lax.all_to_all(pair, "row", 0, 0, axis_index_groups=same_core, tiled=True)
    centroids, copies = new_centroids(parts, old_centroids, list_prior)
    own = lax.all_to_all(copies, "row", 0, 0, axis_index_groups=same_core, tiled=True)
    other = swap(own, "row", n_row, 1)
    rest, sums = residuals(core, list_ids, codes_t, passages, own, other, code_counts(codes_t), n_row, codes)
    parts = lax.all_to_all(sums, "row", 0, 0, tiled=True)
    codebook, copies = new_codebook(parts, old_codebook, code_prior)
    book = lax.all_to_all(copies, "row", 0, 0, tiled=True).reshape(codes, width)
    err = errors(book, codes_t, rest, n_col)
    err = lax.all_to_all(err, "col", 0, 0, tiled=True)
    return centroids, codebook, jnp.sum(err, axis=0).reshape(rows) / D


def solution(mesh):
    in_specs = (P("row", "col"), P("row"), P("row", "col"), P("row", "col"), P("row", "col"))
    out_specs = (P("row", "col"), P("row", "col"), P("row"))
    return jax.shard_map(local, mesh=mesh, in_specs=in_specs, out_specs=out_specs, check_vma=False)
```

```python
import functools
import jax
import jax.numpy as jnp
from jax import lax
from jax.experimental import pallas as pl
from jax.experimental.pallas import tpu as pltpu

from jax.sharding import PartitionSpec as P

D = 1024
LANES = 128
SUB_DIM = 16
NACC = 8
SLAB = 8
K1LIM = 50 * 2**20
RBLOCK = 256
UNROLL = 8
EBLOCK = 512
EPAIRS = 2
VLIM = 24 * 2**20


def sums_kernel(core_ref, ids_hbm, idv_hbm, x_hbm, keep_ref, send_ref, ids, idv, x_ref, lcnt, sems, *accs):
    rows, _ = x_ref.shape
    lists = accs[0].shape[0]
    pieces = keep_ref.shape[0]
    owned = lists // (2 * pieces)
    nchunk = sems.shape[0] - 2
    chunk = rows // nchunk

    def part(c):
        here = pl.ds(c * chunk, chunk)
        return pltpu.make_async_copy(x_hbm.at[here, :], x_ref.at[here, :], sems.at[c])

    fetch_ids = pltpu.make_async_copy(ids_hbm, ids, sems.at[nchunk])
    fetch_idv = pltpu.make_async_copy(idv_hbm, idv, sems.at[nchunk + 1])
    fetch_idv.start()
    fetch_ids.start()
    part(0).start()
    for c in range(1, nchunk):
        part(c).start()

    nhi = lists // LANES
    nt = (((1,), (1,)), ((), ()))

    def counts():
        hi_iota = lax.broadcasted_iota(jnp.int32, (nhi, LANES), 0)
        lo_iota = lax.broadcasted_iota(jnp.int32, (LANES, LANES), 0)
        his, los = [], []
        for t in range(rows // LANES):
            row = idv[t : t + 1, :]
            his.append((lax.shift_right_logical(row, 7) == hi_iota).astype(jnp.bfloat16))
            los.append(((row & (LANES - 1)) == lo_iota).astype(jnp.bfloat16))
        lcnt[...] = lax.dot_general(
            jnp.concatenate(his, 1), jnp.concatenate(los, 1), nt, preferred_element_type=jnp.float32
        )

    def scatter(start):
        for u in range(0, CBLOCK, NACC):
            row = [ids.at[pl.ds(u + j, rows - CBLOCK + 1)][start] for j in range(NACC)]
            old = [accs[j][pl.ds(row[j], 1), :] for j in range(NACC)]
            new = [x_ref[pl.ds(start + u + j, 1), :] for j in range(NACC)]
            for j in range(NACC):
                accs[j][pl.ds(row[j], 1), :] = old[j] + new[j]

    for acc in accs[: NACC // 2]:
        acc[...] = jnp.zeros_like(acc)
    fetch_idv.wait()
    for acc in accs[NACC // 2 :]:
        acc[...] = jnp.zeros_like(acc)
    counts()
    fetch_ids.wait()

    @pl.loop(0, nchunk)
    def _(c):
        part(c).wait()

        @pl.loop(0, chunk // CBLOCK)
        def _(i):
            start = pl.multiple_of(c * chunk + i * CBLOCK, CBLOCK)
            scatter(start)

    core = core_ref[0]
    for out, par in ((send_ref, 1 - core), (keep_ref, core)):
        @pl.loop(0, pieces)
        def _(k):
            owner = 2 * k + par
            start = pl.multiple_of(owner * owned, owned)
            total = accs[0][pl.ds(start, owned), :]
            for acc in accs[1:]:
                total = total + acc[pl.ds(start, owned), :]
            out[k, 0:owned, :] = total
            out[k, pl.ds(owned, SLAB), :] = jnp.concatenate(
                [
                    lcnt[pl.ds(owner * (owned // LANES), owned // LANES), :],
                    jnp.zeros((SLAB - owned // LANES, LANES), jnp.float32),
                ],
                0,
            )


CBLOCK = 1024
NCHUNK = 8


def list_sums(core, ids, x, pieces, lists):
    rows, width = x.shape
    idv = ids.reshape(rows // LANES, LANES)
    ids = pltpu.with_memory_space_constraint(ids, pltpu.HBM)
    idv = pltpu.with_memory_space_constraint(idv, pltpu.HBM)
    owned = lists // (2 * pieces)
    out = jax.ShapeDtypeStruct((pieces, owned + SLAB, width), jnp.float32)
    hbm = pl.BlockSpec(memory_space=pltpu.HBM)
    vmem = pl.BlockSpec(memory_space=pltpu.VMEM)
    return pl.pallas_call(
        sums_kernel,
        in_specs=[pl.BlockSpec(memory_space=pltpu.SMEM)] + [hbm] * 3,
        out_specs=[vmem, vmem],
        out_shape=[out, out],
        scratch_shapes=[
            pltpu.SMEM((rows,), jnp.int32),
            pltpu.VMEM((rows // LANES, LANES), jnp.int32),
            pltpu.VMEM((rows, width), jnp.float32),
            pltpu.VMEM((lists // LANES, LANES), jnp.float32),
            pltpu.SemaphoreType.DMA((NCHUNK + 2,)),
        ]
        + [pltpu.VMEM((lists, width), jnp.float32)] * NACC,
        compiler_params=pltpu.CompilerParams(vmem_limit_bytes=K1LIM),
        name="list_sums",
    )(core, ids, idv, x)


def code_counts_kernel(codes_ref, out_ref):
    subs, rows = codes_ref.shape
    digit = lax.broadcasted_iota(jnp.int32, (SUB_DIM, CBLOCK), 0)
    cc = jnp.zeros((LANES, LANES), jnp.float32)
    for b in range(0, rows, CBLOCK):
        left, right = [], []
        for m in range(subs):
            code = codes_ref[m : m + 1, b : b + CBLOCK]
            left.append((lax.shift_right_logical(code, 4) == digit).astype(jnp.bfloat16))
            right.append(((code & (SUB_DIM - 1)) == digit).astype(jnp.bfloat16))
        cc += lax.dot_general(
            jnp.concatenate(left, 0), jnp.concatenate(right, 0), NT, preferred_element_type=jnp.float32
        )
    r = lax.broadcasted_iota(jnp.int32, cc.shape, 0) // SUB_DIM
    c = lax.broadcasted_iota(jnp.int32, cc.shape, 1) // SUB_DIM
    cc = jnp.where(r == c, cc, 0.0)
    total = cc[0:SUB_DIM, :]
    for m in range(1, subs):
        total = total + cc[m * SUB_DIM : (m + 1) * SUB_DIM, :]
    out_ref[...] = total


def code_counts(codes_t):
    vmem = pl.BlockSpec(memory_space=pltpu.VMEM)
    return pl.pallas_call(
        code_counts_kernel,
        in_specs=[vmem],
        out_specs=vmem,
        out_shape=jax.ShapeDtypeStruct((SUB_DIM, LANES), jnp.float32),
        compiler_params=pltpu.CompilerParams(vmem_limit_bytes=8 * 2**20),
        cost_estimate=pl.CostEstimate(flops=10**9, bytes_accessed=4 * 10**6, transcendentals=0),
        name="code_counts",
    )(codes_t)


def centroid_kernel(prior, part_ref, old_ref, cent_ref, copies_ref):
    owned = old_ref.shape[0]
    total = part_ref[0]
    for k in range(1, part_ref.shape[0]):
        total = total + part_ref[k]
    eye = (
        lax.broadcasted_iota(jnp.int32, (LANES, LANES), 0)
        == lax.broadcasted_iota(jnp.int32, (LANES, LANES), 1)
    )
    for h in range(owned // LANES):
        row = total[owned + h : owned + h + 1, :]
        col = jnp.sum(jnp.where(eye, row, 0.0), axis=1, keepdims=True)
        sl = slice(h * LANES, (h + 1) * LANES)
        cent = (total[sl, :] + prior * old_ref[sl, :]) / (col + prior)
        cent_ref[sl, :] = cent
        for k in range(copies_ref.shape[0]):
            copies_ref[k, sl, :] = cent


def new_centroids(parts, old, prior):
    n = parts.shape[0]
    return pl.pallas_call(
        functools.partial(centroid_kernel, prior),
        out_shape=[
            jax.ShapeDtypeStruct(old.shape, jnp.float32),
            jax.ShapeDtypeStruct((n,) + old.shape, jnp.float32),
        ],
        compiler_params=pltpu.CompilerParams(vmem_limit_bytes=16 * 2**20),
        name="centroids",
    )(parts, old)


NT = (((1,), (1,)), ((), ()))


def resid_kernel(
    core_ref, row_ref, ids_ref, codes_ref, x_ref, own_ref, other_ref, counts_ref, old_ref, rest_ref, keep_ref, send_ref, ids, table, got0, got1, sumst, tall, sems, *, prior
):
    block = got0.shape[0]
    rows = x_ref.shape[0]
    pieces, owned, _ = own_ref.shape
    subs = codes_ref.shape[0]
    owners = counts_ref.shape[0]
    each = old_ref.shape[0]
    half = owners * each // 2
    early, late = pl.ds(0, 2 * block), pl.ds(2 * block, rows - 2 * block)
    fetch = [pltpu.make_async_copy(ids_ref.at[p], ids.at[p], sems.at[n]) for n, p in enumerate((early, late))]
    for f in fetch:
        f.start()
    core = core_ref[0]
    for k in range(pieces):
        table[pl.ds(pl.multiple_of((2 * k + core) * owned, owned), owned), :] = own_ref[k]
        table[pl.ds(pl.multiple_of((2 * k + 1 - core) * owned, owned), owned), :] = other_ref[k]
    sumst[...] = jnp.zeros_like(sumst)
    fetch[0].wait()

    sublane = lax.broadcasted_iota(jnp.int32, (8, LANES), 0)

    def gather(start, got):
        for g in range(0, block, 8):
            tile = None
            for j in range(8):
                row = ids.at[pl.ds(g + j, rows - block + 1)][start]
                line = jnp.broadcast_to(table[pl.ds(row, 1), :], (8, LANES))
                tile = line if j == 0 else jnp.where(sublane == j, line, tile)
            got[g : g + 8, :] = tile

    def work(start, got):
        here = pl.ds(start, block)
        rest = (x_ref[here, :] - got[...]).T
        rest_ref[:, here] = rest
        hi = rest.astype(jnp.bfloat16)
        lo = (rest - hi.astype(jnp.float32)).astype(jnp.bfloat16)
        label = lax.broadcasted_iota(jnp.int32, (half, block), 0)
        for p in range(subs // 2):
            left, right = [], []
            for m in (2 * p, 2 * p + 1):
                code = codes_ref[pl.ds(m, 1), here]
                right.append(((code & (half - 1)) == label).astype(jnp.bfloat16))
                f = slice(m * SUB_DIM, (m + 1) * SUB_DIM)
                both = jnp.concatenate([hi[f], lo[f]], 0)
                top = jnp.broadcast_to((code < half).astype(jnp.bfloat16), both.shape)
                first = both * top
                left += [first, both - first]
            part = lax.dot_general(
                jnp.concatenate(left, 0), jnp.concatenate(right, 0), NT, preferred_element_type=jnp.float32
            )
            for s in range(2):
                f = slice((2 * p + s) * SUB_DIM, (2 * p + s + 1) * SUB_DIM)
                for h in range(2):
                    band = part[(4 * s + 2 * h) * SUB_DIM : (4 * s + 2 * h + 2) * SUB_DIM, s * half : (s + 1) * half]
                    sumst[f, h * half : (h + 1) * half] += band[:SUB_DIM] + band[SUB_DIM:]

    gather(0, got0)
    fetch[1].wait()

    @pl.loop(0, rows // (UNROLL * block))
    def _(i):
        base = pl.multiple_of(i * UNROLL * block, block)
        for u in range(UNROLL):
            now, after = (got0, got1) if u % 2 == 0 else (got1, got0)
            here = pl.multiple_of(base + u * block, block)
            gather(pl.multiple_of(jnp.minimum(here + block, rows - block), block), after)
            work(here, now)

    tall[...] = sumst[...].T
    mine = pl.ds(pl.multiple_of(row_ref[0] * each, each), each)
    tall[mine, :] += prior * old_ref[...]
    for out, parity in ((keep_ref, core), (send_ref, 1 - core)):
        for k in range(owners // 2):
            o = 2 * k + parity
            out[k * each : (k + 1) * each, :] = tall[pl.ds(pl.multiple_of(o * each, each), each), :]
            out[pl.ds(owners // 2 * each + k, 1), :] = counts_ref[pl.ds(o, 1), :]


def residuals(core, row, ids, codes_t, x, own, other, counts, old, owners, prior, block=RBLOCK):
    codes = owners * old.shape[0]
    half = jax.ShapeDtypeStruct((codes // 2 + owners // 2, x.shape[1]), jnp.float32)
    rows, width = x.shape
    pieces, owned, _ = own.shape
    vmem = pl.BlockSpec(memory_space=pltpu.VMEM)
    return pl.pallas_call(
        functools.partial(resid_kernel, prior=prior),
        in_specs=[pl.BlockSpec(memory_space=pltpu.SMEM)] * 2 + [vmem] * 7,
        out_specs=[vmem] * 3,
        out_shape=[
            jax.ShapeDtypeStruct((width, rows), jnp.float32),
            half,
            half,
        ],
        scratch_shapes=[
            pltpu.SMEM((rows,), jnp.int32),
            pltpu.VMEM((2 * pieces * owned, width), jnp.float32),
            pltpu.VMEM((block, width), jnp.float32),
            pltpu.VMEM((block, width), jnp.float32),
            pltpu.VMEM((width, codes), jnp.float32),
            pltpu.VMEM((codes, width), jnp.float32),
            pltpu.SemaphoreType.DMA((2,)),
        ],
        compiler_params=pltpu.CompilerParams(vmem_limit_bytes=VLIM),
        name="residuals",
    )(core, row, ids, codes_t, x, own, other, counts, old)


def book_bands(book_t, pair):
    half = book_t.shape[1] // 2
    bands = []
    for s in range(2):
        f = slice((2 * pair + s) * SUB_DIM, (2 * pair + s + 1) * SUB_DIM)
        for h in range(2):
            words = book_t[f, h * half : (h + 1) * half]
            hi = words.astype(jnp.bfloat16)
            lo = (words - hi.astype(jnp.float32)).astype(jnp.bfloat16)
            none = jnp.zeros_like(hi)
            bands += [jnp.concatenate([p, none] if s == 0 else [none, p], 1) for p in (hi, lo)]
    return jnp.concatenate(bands, 0)


def whole_book(prior, core_ref, own_ref, other_ref, each, book_ref, counts_ref):
    owners = book_ref.shape[0] // each
    core = core_ref[0]
    for src, parity in ((own_ref, core), (other_ref, 1 - core)):
        for k in range(owners // 2):
            o = 2 * k + parity
            book_ref[pl.ds(pl.multiple_of(o * each, each), each), :] = src[k * each : (k + 1) * each, :]
            counts_ref[pl.ds(o, 1), :] = src[pl.ds(owners // 2 * each + k, 1), :]
    lane = lax.broadcasted_iota(jnp.int32, (each, LANES), 1)
    code = lax.broadcasted_iota(jnp.int32, (each, LANES), 0)
    keep = (lane & (SUB_DIM - 1)) == code
    whole = counts_ref[...].astype(jnp.int32)
    digits = [lax.shift_right_logical(whole, 12), lax.shift_right_logical(whole, 6) & 63, whole & 63]
    picked = jnp.concatenate(
        [
            jnp.concatenate([jnp.where(keep, d[o : o + 1, :], 0) for o in range(owners)], 0).astype(jnp.bfloat16)
            for d in digits
        ],
        1,
    )
    r = lax.broadcasted_iota(jnp.int32, (LANES, LANES), 0) // SUB_DIM
    c = lax.broadcasted_iota(jnp.int32, (LANES, LANES), 1) // SUB_DIM
    ones = jnp.concatenate([jnp.where(r == c, w, 0.0).astype(jnp.bfloat16) for w in (4096.0, 64.0, 1.0)], 0)
    spread = jnp.dot(picked, ones, preferred_element_type=jnp.float32)
    book_ref[...] = book_ref[...] / (spread + prior)


def errors_kernel(core_ref, row_ref, own_ref, other_ref, codes_ref, rest_ref, out_ref, mine_ref, table, bands, book_ref, counts_ref, *, prior):
    subs, rows = codes_ref.shape
    half = book_ref.shape[0] // 2
    each = mine_ref.shape[0]
    whole_book(prior, core_ref, own_ref, other_ref, each, book_ref, counts_ref)
    mine_ref[...] = book_ref[pl.ds(pl.multiple_of(row_ref[0] * each, each), each), :]
    by_product = bands.shape[0]
    looked_up = subs - 2 * by_product

    table[...] = book_ref[...].T
    for q in range(by_product):
        bands[q] = book_bands(table[...], looked_up // 2 + q)
    label = lax.broadcasted_iota(jnp.int32, (half, EBLOCK), 0)

    def product(here):
        acc = jnp.zeros((8, EBLOCK), jnp.float32)
        for q in range(by_product):
            m0 = looked_up + 2 * q
            code = [codes_ref[m : m + 1, here] for m in (m0, m0 + 1)]
            hot = [((c & (half - 1)) == label).astype(jnp.bfloat16) for c in code]
            part = jnp.dot(bands[q], jnp.concatenate(hot, 0), preferred_element_type=jnp.float32)
            for s in range(2):
                p = [part[(4 * s + b) * SUB_DIM : (4 * s + b + 1) * SUB_DIM, :] for b in range(4)]
                word = jnp.where(jnp.broadcast_to(code[s] < half, p[0].shape), p[0] + p[1], p[2] + p[3])
                d = rest_ref[(m0 + s) * SUB_DIM : (m0 + s + 1) * SUB_DIM, here] - word
                d = d * d
                for g in range(0, SUB_DIM, 8):
                    acc = acc + d[g : g + 8, :]
        return acc

    def lookup(cols):
        acc = jnp.zeros((8, LANES), jnp.float32)
        for m in range(looked_up):
            idx = jnp.broadcast_to(codes_ref[m : m + 1, cols], (8, LANES))
            low = idx & (half - 1)
            first = idx < half
            for g in range(0, SUB_DIM, 8):
                f = slice(m * SUB_DIM + g, m * SUB_DIM + g + 8)
                a = jnp.take_along_axis(table[f, 0:half], low, axis=1)
                b = jnp.take_along_axis(table[f, half : 2 * half], low, axis=1)
                d = rest_ref[f, cols] - jnp.where(first, a, b)
                acc = acc + d * d
        return acc

    for b in range(0, rows, EBLOCK):
        wide = product(slice(b, b + EBLOCK))
        for t in range(0, EBLOCK, LANES):
            acc = wide[:, t : t + LANES] + lookup(slice(b + t, b + t + LANES))
            row = jnp.sum(acc, axis=0, keepdims=True)
            at = (b + t) // LANES
            for k in range(out_ref.shape[0]):
                out_ref[k, at : at + 1, :] = row


def errors(core, row, own, other, codes_t, rest, copies, owned, owners, prior):
    width, rows = rest.shape
    codes = owned * owners
    vmem = pl.BlockSpec(memory_space=pltpu.VMEM)
    return pl.pallas_call(
        functools.partial(errors_kernel, prior=prior),
        in_specs=[pl.BlockSpec(memory_space=pltpu.SMEM)] * 2 + [vmem] * 4,
        out_specs=[vmem] * 2,
        out_shape=[
            jax.ShapeDtypeStruct((copies, rows // LANES, LANES), jnp.float32),
            jax.ShapeDtypeStruct((owned, width), jnp.float32),
        ],
        scratch_shapes=[
            pltpu.VMEM((width, codes), jnp.float32),
            pltpu.VMEM((EPAIRS, LANES, codes), jnp.bfloat16),
            pltpu.VMEM((codes, width), jnp.float32),
            pltpu.VMEM((owners, width), jnp.float32),
        ],
        compiler_params=pltpu.CompilerParams(vmem_limit_bytes=24 * 2**20),
        name="errors",
    )(core, row, own, other, codes_t, rest)


def swap(x, axis, n, bit):
    return lax.ppermute(x, axis, [(i, i ^ bit) for i in range(n)])


def local(passages, list_ids, code_ids, old_centroids, old_codebook):
    rows, width = passages.shape
    n_row = lax.axis_size("row")
    n_col = lax.axis_size("col")
    total = rows * n_row
    owned_lists = old_centroids.shape[0]
    owned_codes = old_codebook.shape[0]
    lists = owned_lists * n_row
    codes = owned_codes * n_row
    list_prior = float(total // lists)
    code_prior = float(total // codes)
    pieces = n_row // 2
    same_core = [[2 * k + c for k in range(pieces)] for c in range(2)]
    row = lax.axis_index("row").astype(jnp.int32).reshape(1)
    core = (lax.axis_index("row") % 2).astype(jnp.int32).reshape(1)
    codes_t = code_ids.T

    keep, send = list_sums(core, list_ids, passages, pieces, lists)
    pair = keep + swap(send, "row", n_row, 1)
    parts = lax.all_to_all(pair, "row", 0, 0, axis_index_groups=same_core, tiled=True)
    centroids, copies = new_centroids(parts, old_centroids, list_prior)
    own = lax.all_to_all(copies, "row", 0, 0, axis_index_groups=same_core, tiled=True)
    other = swap(own, "row", n_row, 1)
    rest, keep, send = residuals(
        core, row, list_ids, codes_t, passages, own, other, code_counts(codes_t), old_codebook, n_row, code_prior
    )
    half = keep + swap(send, "row", n_row, 1)
    bit = n_row // 2
    while bit > 1:
        half = half + swap(half, "row", n_row, bit)
        bit //= 2
    err, codebook = errors(
        core, row, half, swap(half, "row", n_row, 1), codes_t, rest, n_col, owned_codes, n_row, code_prior
    )
    err = lax.all_to_all(err, "col", 0, 0, tiled=True)
    return centroids, codebook, jnp.sum(err, axis=0).reshape(rows) / D


def solution(mesh):
    in_specs = (P("row", "col"), P("row"), P("row", "col"), P("row", "col"), P("row", "col"))
    out_specs = (P("row", "col"), P("row", "col"), P("row"))
    return jax.shard_map(local, mesh=mesh, in_specs=in_specs, out_specs=out_specs, check_vma=False)
```

```python
import functools
import jax
import jax.numpy as jnp
from jax import lax
from jax.experimental import pallas as pl
from jax.experimental.pallas import tpu as pltpu

from jax.sharding import PartitionSpec as P

D = 1024
LANES = 128
SUB_DIM = 16
NACC = 8
SLAB = 8
K1LIM = 50 * 2**20
RBLOCK = 256
UNROLL = 8
EBLOCK = 512
EPAIRS = 2
VLIM = 24 * 2**20


def sums_kernel(core_ref, ids_hbm, idv_hbm, x_hbm, keep_ref, send_ref, ids, idv, x_ref, lcnt, sems, *accs):
    rows, _ = x_ref.shape
    lists = accs[0].shape[0]
    pieces = keep_ref.shape[0]
    owned = lists // (2 * pieces)
    nchunk = sems.shape[0] - 2
    chunk = rows // nchunk

    def part(c):
        here = pl.ds(c * chunk, chunk)
        return pltpu.make_async_copy(x_hbm.at[here, :], x_ref.at[here, :], sems.at[c])

    fetch_ids = pltpu.make_async_copy(ids_hbm, ids, sems.at[nchunk])
    fetch_idv = pltpu.make_async_copy(idv_hbm, idv, sems.at[nchunk + 1])
    fetch_idv.start()
    fetch_ids.start()
    part(0).start()
    for c in range(1, nchunk):
        part(c).start()

    nhi = lists // LANES
    nt = (((1,), (1,)), ((), ()))

    def counts():
        hi_iota = lax.broadcasted_iota(jnp.int32, (nhi, LANES), 0)
        lo_iota = lax.broadcasted_iota(jnp.int32, (LANES, LANES), 0)
        his, los = [], []
        for t in range(rows // LANES):
            row = idv[t : t + 1, :]
            his.append((lax.shift_right_logical(row, 7) == hi_iota).astype(jnp.bfloat16))
            los.append(((row & (LANES - 1)) == lo_iota).astype(jnp.bfloat16))
        lcnt[...] = lax.dot_general(
            jnp.concatenate(his, 1), jnp.concatenate(los, 1), nt, preferred_element_type=jnp.float32
        )

    def scatter(start):
        for u in range(0, CBLOCK, NACC):
            row = [ids.at[pl.ds(u + j, rows - CBLOCK + 1)][start] for j in range(NACC)]
            old = [accs[j][pl.ds(row[j], 1), :] for j in range(NACC)]
            new = [x_ref[pl.ds(start + u + j, 1), :] for j in range(NACC)]
            for j in range(NACC):
                accs[j][pl.ds(row[j], 1), :] = old[j] + new[j]

    for acc in accs[: NACC // 2]:
        acc[...] = jnp.zeros_like(acc)
    fetch_idv.wait()
    for acc in accs[NACC // 2 :]:
        acc[...] = jnp.zeros_like(acc)
    counts()
    fetch_ids.wait()

    @pl.loop(0, nchunk)
    def _(c):
        part(c).wait()

        @pl.loop(0, chunk // CBLOCK)
        def _(i):
            start = pl.multiple_of(c * chunk + i * CBLOCK, CBLOCK)
            scatter(start)

    core = core_ref[0]
    for out, par in ((send_ref, 1 - core), (keep_ref, core)):
        @pl.loop(0, pieces)
        def _(k):
            owner = 2 * k + par
            start = pl.multiple_of(owner * owned, owned)
            total = accs[0][pl.ds(start, owned), :]
            for acc in accs[1:]:
                total = total + acc[pl.ds(start, owned), :]
            out[k, 0:owned, :] = total
            out[k, pl.ds(owned, SLAB), :] = jnp.concatenate(
                [
                    lcnt[pl.ds(owner * (owned // LANES), owned // LANES), :],
                    jnp.zeros((SLAB - owned // LANES, LANES), jnp.float32),
                ],
                0,
            )


CBLOCK = 1024
NCHUNK = 8


def list_sums(core, ids, x, pieces, lists):
    rows, width = x.shape
    idv = ids.reshape(rows // LANES, LANES)
    ids = pltpu.with_memory_space_constraint(ids, pltpu.HBM)
    idv = pltpu.with_memory_space_constraint(idv, pltpu.HBM)
    owned = lists // (2 * pieces)
    out = jax.ShapeDtypeStruct((pieces, owned + SLAB, width), jnp.float32)
    hbm = pl.BlockSpec(memory_space=pltpu.HBM)
    vmem = pl.BlockSpec(memory_space=pltpu.VMEM)
    return pl.pallas_call(
        sums_kernel,
        in_specs=[pl.BlockSpec(memory_space=pltpu.SMEM)] + [hbm] * 3,
        out_specs=[vmem, vmem],
        out_shape=[out, out],
        scratch_shapes=[
            pltpu.SMEM((rows,), jnp.int32),
            pltpu.VMEM((rows // LANES, LANES), jnp.int32),
            pltpu.VMEM((rows, width), jnp.float32),
            pltpu.VMEM((lists // LANES, LANES), jnp.float32),
            pltpu.SemaphoreType.DMA((NCHUNK + 2,)),
        ]
        + [pltpu.VMEM((lists, width), jnp.float32)] * NACC,
        compiler_params=pltpu.CompilerParams(vmem_limit_bytes=K1LIM),
        name="list_sums",
    )(core, ids, idv, x)


def code_counts_kernel(codes_ref, out_ref):
    subs, rows = codes_ref.shape
    digit = lax.broadcasted_iota(jnp.int32, (SUB_DIM, CBLOCK), 0)
    cc = jnp.zeros((LANES, LANES), jnp.float32)
    for b in range(0, rows, CBLOCK):
        left, right = [], []
        for m in range(subs):
            code = codes_ref[m : m + 1, b : b + CBLOCK]
            left.append((lax.shift_right_logical(code, 4) == digit).astype(jnp.bfloat16))
            right.append(((code & (SUB_DIM - 1)) == digit).astype(jnp.bfloat16))
        cc += lax.dot_general(
            jnp.concatenate(left, 0), jnp.concatenate(right, 0), NT, preferred_element_type=jnp.float32
        )
    r = lax.broadcasted_iota(jnp.int32, cc.shape, 0) // SUB_DIM
    c = lax.broadcasted_iota(jnp.int32, cc.shape, 1) // SUB_DIM
    cc = jnp.where(r == c, cc, 0.0)
    total = cc[0:SUB_DIM, :]
    for m in range(1, subs):
        total = total + cc[m * SUB_DIM : (m + 1) * SUB_DIM, :]
    out_ref[...] = total


def code_counts(codes_t):
    vmem = pl.BlockSpec(memory_space=pltpu.VMEM)
    return pl.pallas_call(
        code_counts_kernel,
        in_specs=[vmem],
        out_specs=vmem,
        out_shape=jax.ShapeDtypeStruct((SUB_DIM, LANES), jnp.float32),
        compiler_params=pltpu.CompilerParams(vmem_limit_bytes=8 * 2**20),
        cost_estimate=pl.CostEstimate(flops=10**9, bytes_accessed=4 * 10**6, transcendentals=0),
        name="code_counts",
    )(codes_t)


def centroid_kernel(prior, part_ref, old_ref, cent_ref, copies_ref):
    owned = old_ref.shape[0]
    total = part_ref[0]
    for k in range(1, part_ref.shape[0]):
        total = total + part_ref[k]
    eye = (
        lax.broadcasted_iota(jnp.int32, (LANES, LANES), 0)
        == lax.broadcasted_iota(jnp.int32, (LANES, LANES), 1)
    )
    for h in range(owned // LANES):
        row = total[owned + h : owned + h + 1, :]
        col = jnp.sum(jnp.where(eye, row, 0.0), axis=1, keepdims=True)
        sl = slice(h * LANES, (h + 1) * LANES)
        cent = (total[sl, :] + prior * old_ref[sl, :]) / (col + prior)
        cent_ref[sl, :] = cent
        for k in range(copies_ref.shape[0]):
            copies_ref[k, sl, :] = cent


def new_centroids(parts, old, prior):
    n = parts.shape[0]
    return pl.pallas_call(
        functools.partial(centroid_kernel, prior),
        out_shape=[
            jax.ShapeDtypeStruct(old.shape, jnp.float32),
            jax.ShapeDtypeStruct((n,) + old.shape, jnp.float32),
        ],
        compiler_params=pltpu.CompilerParams(vmem_limit_bytes=16 * 2**20),
        name="centroids",
    )(parts, old)


NT = (((1,), (1,)), ((), ()))


def resid_kernel(
    core_ref, row_ref, ids_ref, codes_ref, x_ref, own_ref, other_ref, counts_ref, old_ref, rest_ref, keep_ref, send_ref, ids, table, got0, got1, sumst, tall, sems, *, prior
):
    block = got0.shape[0]
    rows = x_ref.shape[0]
    pieces, owned, _ = own_ref.shape
    subs = codes_ref.shape[0]
    owners = counts_ref.shape[0]
    each = old_ref.shape[0]
    half = owners * each // 2
    early, late = pl.ds(0, 2 * block), pl.ds(2 * block, rows - 2 * block)
    fetch = [pltpu.make_async_copy(ids_ref.at[p], ids.at[p], sems.at[n]) for n, p in enumerate((early, late))]
    for f in fetch:
        f.start()
    core = core_ref[0]
    for k in range(pieces):
        table[pl.ds(pl.multiple_of((2 * k + core) * owned, owned), owned), :] = own_ref[k]
        table[pl.ds(pl.multiple_of((2 * k + 1 - core) * owned, owned), owned), :] = other_ref[k]
    sumst[...] = jnp.zeros_like(sumst)
    fetch[0].wait()

    sublane = lax.broadcasted_iota(jnp.int32, (8, LANES), 0)

    def gather(start, got):
        for g in range(0, block, 8):
            tile = None
            for j in range(8):
                row = ids.at[pl.ds(g + j, rows - block + 1)][start]
                line = jnp.broadcast_to(table[pl.ds(row, 1), :], (8, LANES))
                tile = line if j == 0 else jnp.where(sublane == j, line, tile)
            got[g : g + 8, :] = tile

    def work(start, got):
        here = pl.ds(start, block)
        rest = (x_ref[here, :] - got[...]).T
        rest_ref[:, here] = rest
        hi = rest.astype(jnp.bfloat16)
        lo = (rest - hi.astype(jnp.float32)).astype(jnp.bfloat16)
        label = lax.broadcasted_iota(jnp.int32, (half, block), 0)
        for p in range(subs // 2):
            left, right = [], []
            for m in (2 * p, 2 * p + 1):
                code = codes_ref[pl.ds(m, 1), here]
                right.append(((code & (half - 1)) == label).astype(jnp.bfloat16))
                f = slice(m * SUB_DIM, (m + 1) * SUB_DIM)
                both = jnp.concatenate([hi[f], lo[f]], 0)
                top = jnp.broadcast_to((code < half).astype(jnp.bfloat16), both.shape)
                first = both * top
                left += [first, both - first]
            part = lax.dot_general(
                jnp.concatenate(left, 0), jnp.concatenate(right, 0), NT, preferred_element_type=jnp.float32
            )
            for s in range(2):
                f = slice((2 * p + s) * SUB_DIM, (2 * p + s + 1) * SUB_DIM)
                for h in range(2):
                    band = part[(4 * s + 2 * h) * SUB_DIM : (4 * s + 2 * h + 2) * SUB_DIM, s * half : (s + 1) * half]
                    sumst[f, h * half : (h + 1) * half] += band[:SUB_DIM] + band[SUB_DIM:]

    gather(0, got0)
    fetch[1].wait()

    @pl.loop(0, rows // (UNROLL * block))
    def _(i):
        base = pl.multiple_of(i * UNROLL * block, block)
        for u in range(UNROLL):
            now, after = (got0, got1) if u % 2 == 0 else (got1, got0)
            here = pl.multiple_of(base + u * block, block)
            gather(pl.multiple_of(jnp.minimum(here + block, rows - block), block), after)
            work(here, now)

    tall[...] = sumst[...].T
    mine = pl.ds(pl.multiple_of(row_ref[0] * each, each), each)
    tall[mine, :] += prior * old_ref[...]
    for out, parity in ((keep_ref, core), (send_ref, 1 - core)):
        for k in range(owners // 2):
            o = 2 * k + parity
            out[k * each : (k + 1) * each, :] = tall[pl.ds(pl.multiple_of(o * each, each), each), :]
            out[pl.ds(owners // 2 * each + k, 1), :] = counts_ref[pl.ds(o, 1), :]


def residuals(core, row, ids, codes_t, x, own, other, counts, old, owners, prior, block=RBLOCK):
    codes = owners * old.shape[0]
    half = jax.ShapeDtypeStruct((codes // 2 + owners // 2, x.shape[1]), jnp.float32)
    rows, width = x.shape
    pieces, owned, _ = own.shape
    vmem = pl.BlockSpec(memory_space=pltpu.VMEM)
    return pl.pallas_call(
        functools.partial(resid_kernel, prior=prior),
        in_specs=[pl.BlockSpec(memory_space=pltpu.SMEM)] * 2 + [vmem] * 7,
        out_specs=[vmem] * 3,
        out_shape=[
            jax.ShapeDtypeStruct((width, rows), jnp.float32),
            half,
            half,
        ],
        scratch_shapes=[
            pltpu.SMEM((rows,), jnp.int32),
            pltpu.VMEM((2 * pieces * owned, width), jnp.float32),
            pltpu.VMEM((block, width), jnp.float32),
            pltpu.VMEM((block, width), jnp.float32),
            pltpu.VMEM((width, codes), jnp.float32),
            pltpu.VMEM((codes, width), jnp.float32),
            pltpu.SemaphoreType.DMA((2,)),
        ],
        compiler_params=pltpu.CompilerParams(vmem_limit_bytes=VLIM),
        name="residuals",
    )(core, row, ids, codes_t, x, own, other, counts, old)


def book_bands(book_t, pair):
    half = book_t.shape[1] // 2
    bands = []
    for s in range(2):
        f = slice((2 * pair + s) * SUB_DIM, (2 * pair + s + 1) * SUB_DIM)
        for h in range(2):
            words = book_t[f, h * half : (h + 1) * half]
            hi = words.astype(jnp.bfloat16)
            lo = (words - hi.astype(jnp.float32)).astype(jnp.bfloat16)
            none = jnp.zeros_like(hi)
            bands += [jnp.concatenate([p, none] if s == 0 else [none, p], 1) for p in (hi, lo)]
    return jnp.concatenate(bands, 0)


def whole_book(prior, core_ref, own_ref, other_ref, each, book_ref, counts_ref):
    owners = book_ref.shape[0] // each
    core = core_ref[0]
    for src, parity in ((own_ref, core), (other_ref, 1 - core)):
        for k in range(owners // 2):
            o = 2 * k + parity
            book_ref[pl.ds(pl.multiple_of(o * each, each), each), :] = src[k * each : (k + 1) * each, :]
            counts_ref[pl.ds(o, 1), :] = src[pl.ds(owners // 2 * each + k, 1), :]
    lane = lax.broadcasted_iota(jnp.int32, (each, LANES), 1)
    code = lax.broadcasted_iota(jnp.int32, (each, LANES), 0)
    keep = (lane & (SUB_DIM - 1)) == code
    whole = counts_ref[...].astype(jnp.int32)
    digits = [lax.shift_right_logical(whole, 12), lax.shift_right_logical(whole, 6) & 63, whole & 63]
    picked = jnp.concatenate(
        [
            jnp.concatenate([jnp.where(keep, d[o : o + 1, :], 0) for o in range(owners)], 0).astype(jnp.bfloat16)
            for d in digits
        ],
        1,
    )
    r = lax.broadcasted_iota(jnp.int32, (LANES, LANES), 0) // SUB_DIM
    c = lax.broadcasted_iota(jnp.int32, (LANES, LANES), 1) // SUB_DIM
    ones = jnp.concatenate([jnp.where(r == c, w, 0.0).astype(jnp.bfloat16) for w in (4096.0, 64.0, 1.0)], 0)
    spread = jnp.dot(picked, ones, preferred_element_type=jnp.float32)
    book_ref[...] = book_ref[...] / (spread + prior)


def errors_kernel(core_ref, row_ref, own_ref, other_ref, codes_ref, rest_ref, out_ref, mine_ref, table, bands, book_ref, counts_ref, *, prior):
    subs, rows = codes_ref.shape
    half = book_ref.shape[0] // 2
    each = mine_ref.shape[0]
    whole_book(prior, core_ref, own_ref, other_ref, each, book_ref, counts_ref)
    mine_ref[...] = book_ref[pl.ds(pl.multiple_of(row_ref[0] * each, each), each), :]
    by_product = bands.shape[0]
    looked_up = subs - 2 * by_product

    table[...] = book_ref[...].T
    for q in range(by_product):
        bands[q] = book_bands(table[...], looked_up // 2 + q)
    label = lax.broadcasted_iota(jnp.int32, (half, EBLOCK), 0)

    def product(here):
        acc = jnp.zeros((8, EBLOCK), jnp.float32)
        for q in range(by_product):
            m0 = looked_up + 2 * q
            code = [codes_ref[m : m + 1, here] for m in (m0, m0 + 1)]
            hot = [((c & (half - 1)) == label).astype(jnp.bfloat16) for c in code]
            part = jnp.dot(bands[q], jnp.concatenate(hot, 0), preferred_element_type=jnp.float32)
            for s in range(2):
                p = [part[(4 * s + b) * SUB_DIM : (4 * s + b + 1) * SUB_DIM, :] for b in range(4)]
                word = jnp.where(jnp.broadcast_to(code[s] < half, p[0].shape), p[0] + p[1], p[2] + p[3])
                d = rest_ref[(m0 + s) * SUB_DIM : (m0 + s + 1) * SUB_DIM, here] - word
                d = d * d
                for g in range(0, SUB_DIM, 8):
                    acc = acc + d[g : g + 8, :]
        return acc

    def lookup(cols):
        acc = jnp.zeros((8, LANES), jnp.float32)
        for m in range(looked_up):
            idx = jnp.broadcast_to(codes_ref[m : m + 1, cols], (8, LANES))
            low = idx & (half - 1)
            first = idx < half
            for g in range(0, SUB_DIM, 8):
                f = slice(m * SUB_DIM + g, m * SUB_DIM + g + 8)
                a = jnp.take_along_axis(table[f, 0:half], low, axis=1)
                b = jnp.take_along_axis(table[f, half : 2 * half], low, axis=1)
                d = rest_ref[f, cols] - jnp.where(first, a, b)
                acc = acc + d * d
        return acc

    for b in range(0, rows, EBLOCK):
        wide = product(slice(b, b + EBLOCK))
        for t in range(0, EBLOCK, LANES):
            acc = wide[:, t : t + LANES] + lookup(slice(b + t, b + t + LANES))
            row = jnp.sum(acc, axis=0, keepdims=True)
            at = (b + t) // LANES
            for k in range(out_ref.shape[0]):
                out_ref[k, at : at + 1, :] = row


def errors(core, row, own, other, codes_t, rest, copies, owned, owners, prior):
    width, rows = rest.shape
    codes = owned * owners
    vmem = pl.BlockSpec(memory_space=pltpu.VMEM)
    return pl.pallas_call(
        functools.partial(errors_kernel, prior=prior),
        in_specs=[pl.BlockSpec(memory_space=pltpu.SMEM)] * 2 + [vmem] * 4,
        out_specs=[vmem] * 2,
        out_shape=[
            jax.ShapeDtypeStruct((copies, rows // LANES, LANES), jnp.float32),
            jax.ShapeDtypeStruct((owned, width), jnp.float32),
        ],
        scratch_shapes=[
            pltpu.VMEM((width, codes), jnp.float32),
            pltpu.VMEM((EPAIRS, LANES, codes), jnp.bfloat16),
            pltpu.VMEM((codes, width), jnp.float32),
            pltpu.VMEM((owners, width), jnp.float32),
        ],
        compiler_params=pltpu.CompilerParams(vmem_limit_bytes=24 * 2**20),
        name="errors",
    )(core, row, own, other, codes_t, rest)


def swap(x, axis, n, bit):
    return lax.ppermute(x, axis, [(i, i ^ bit) for i in range(n)])


def turned(x, axis, n, ring, step):
    def there(i):
        y, at, core = i // (2 * ring), i // 2 % ring, i % 2
        return (y * ring + (at + step) % ring) * 2 + core

    return lax.ppermute(x, axis, [(i, there(i)) for i in range(n)])


def local(passages, list_ids, code_ids, old_centroids, old_codebook):
    rows, width = passages.shape
    n_row = lax.axis_size("row")
    n_col = lax.axis_size("col")
    total = rows * n_row
    owned_lists = old_centroids.shape[0]
    owned_codes = old_codebook.shape[0]
    lists = owned_lists * n_row
    codes = owned_codes * n_row
    list_prior = float(total // lists)
    code_prior = float(total // codes)
    pieces = n_row // 2
    same_core = [[2 * k + c for k in range(pieces)] for c in range(2)]
    row = lax.axis_index("row").astype(jnp.int32).reshape(1)
    core = (lax.axis_index("row") % 2).astype(jnp.int32).reshape(1)
    codes_t = code_ids.T

    keep, send = list_sums(core, list_ids, passages, pieces, lists)
    pair = keep + swap(send, "row", n_row, 1)
    parts = lax.all_to_all(pair, "row", 0, 0, axis_index_groups=same_core, tiled=True)
    centroids, copies = new_centroids(parts, old_centroids, list_prior)
    own = lax.all_to_all(copies, "row", 0, 0, axis_index_groups=same_core, tiled=True)
    other = swap(own, "row", n_row, 1)
    rest, keep, send = residuals(
        core, row, list_ids, codes_t, passages, own, other, code_counts(codes_t), old_codebook, n_row, code_prior
    )
    half = keep + swap(send, "row", n_row, 1)
    half = half + swap(half, "row", n_row, n_row // 2)
    ring = n_row // 4
    half = half + sum(turned(half, "row", n_row, ring, step) for step in range(1, ring))
    err, codebook = errors(
        core, row, half, swap(half, "row", n_row, 1), codes_t, rest, n_col, owned_codes, n_row, code_prior
    )
    err = lax.all_to_all(err, "col", 0, 0, tiled=True)
    return centroids, codebook, jnp.sum(err, axis=0).reshape(rows) / D


def solution(mesh):
    in_specs = (P("row", "col"), P("row"), P("row", "col"), P("row", "col"), P("row", "col"))
    out_specs = (P("row", "col"), P("row", "col"), P("row"))
    return jax.shard_map(local, mesh=mesh, in_specs=in_specs, out_specs=out_specs, check_vma=False)
```

```python
import functools
import jax
import jax.numpy as jnp
from jax import lax
from jax.experimental import pallas as pl
from jax.experimental.pallas import tpu as pltpu

from jax.sharding import PartitionSpec as P

D = 1024
LANES = 128
SUB_DIM = 16
NACC = 8
SLAB = 8
K1LIM = 50 * 2**20
RBLOCK = 256
UNROLL = 8
EBLOCK = 512
EPAIRS = 2
VLIM = 24 * 2**20


def sums_kernel(core_ref, ids_hbm, idv_hbm, x_hbm, keep_ref, send_ref, ids, idv, x_ref, lcnt, sems, *accs):
    rows, _ = x_ref.shape
    lists = accs[0].shape[0]
    pieces = keep_ref.shape[0]
    owned = lists // (2 * pieces)
    nchunk = sems.shape[0] - 2
    chunk = rows // nchunk

    def part(c):
        here = pl.ds(c * chunk, chunk)
        return pltpu.make_async_copy(x_hbm.at[here, :], x_ref.at[here, :], sems.at[c])

    fetch_ids = pltpu.make_async_copy(ids_hbm, ids, sems.at[nchunk])
    fetch_idv = pltpu.make_async_copy(idv_hbm, idv, sems.at[nchunk + 1])
    fetch_idv.start()
    fetch_ids.start()
    part(0).start()
    for c in range(1, nchunk):
        part(c).start()

    nhi = lists // LANES
    nt = (((1,), (1,)), ((), ()))

    def counts():
        hi_iota = lax.broadcasted_iota(jnp.int32, (nhi, LANES), 0)
        lo_iota = lax.broadcasted_iota(jnp.int32, (LANES, LANES), 0)
        his, los = [], []
        for t in range(rows // LANES):
            row = idv[t : t + 1, :]
            his.append((lax.shift_right_logical(row, 7) == hi_iota).astype(jnp.bfloat16))
            los.append(((row & (LANES - 1)) == lo_iota).astype(jnp.bfloat16))
        lcnt[...] = lax.dot_general(
            jnp.concatenate(his, 1), jnp.concatenate(los, 1), nt, preferred_element_type=jnp.float32
        )

    def scatter(start):
        for u in range(0, CBLOCK, NACC):
            row = [ids.at[pl.ds(u + j, rows - CBLOCK + 1)][start] for j in range(NACC)]
            old = [accs[j][pl.ds(row[j], 1), :] for j in range(NACC)]
            new = [x_ref[pl.ds(start + u + j, 1), :] for j in range(NACC)]
            for j in range(NACC):
                accs[j][pl.ds(row[j], 1), :] = old[j] + new[j]

    for acc in accs[: NACC // 2]:
        acc[...] = jnp.zeros_like(acc)
    fetch_idv.wait()
    for acc in accs[NACC // 2 :]:
        acc[...] = jnp.zeros_like(acc)
    counts()
    fetch_ids.wait()

    @pl.loop(0, nchunk)
    def _(c):
        part(c).wait()

        @pl.loop(0, chunk // CBLOCK)
        def _(i):
            start = pl.multiple_of(c * chunk + i * CBLOCK, CBLOCK)
            scatter(start)

    core = core_ref[0]
    for out, par in ((send_ref, 1 - core), (keep_ref, core)):
        @pl.loop(0, pieces)
        def _(k):
            owner = 2 * k + par
            start = pl.multiple_of(owner * owned, owned)
            total = accs[0][pl.ds(start, owned), :]
            for acc in accs[1:]:
                total = total + acc[pl.ds(start, owned), :]
            out[k, 0:owned, :] = total
            out[k, pl.ds(owned, SLAB), :] = jnp.concatenate(
                [
                    lcnt[pl.ds(owner * (owned // LANES), owned // LANES), :],
                    jnp.zeros((SLAB - owned // LANES, LANES), jnp.float32),
                ],
                0,
            )


CBLOCK = 1024
NCHUNK = 8


def list_sums(core, ids, x, pieces, lists):
    rows, width = x.shape
    idv = ids.reshape(rows // LANES, LANES)
    ids = pltpu.with_memory_space_constraint(ids, pltpu.HBM)
    idv = pltpu.with_memory_space_constraint(idv, pltpu.HBM)
    owned = lists // (2 * pieces)
    out = jax.ShapeDtypeStruct((pieces, owned + SLAB, width), jnp.float32)
    hbm = pl.BlockSpec(memory_space=pltpu.HBM)
    vmem = pl.BlockSpec(memory_space=pltpu.VMEM)
    return pl.pallas_call(
        sums_kernel,
        in_specs=[pl.BlockSpec(memory_space=pltpu.SMEM)] + [hbm] * 3,
        out_specs=[vmem, vmem],
        out_shape=[out, out],
        scratch_shapes=[
            pltpu.SMEM((rows,), jnp.int32),
            pltpu.VMEM((rows // LANES, LANES), jnp.int32),
            pltpu.VMEM((rows, width), jnp.float32),
            pltpu.VMEM((lists // LANES, LANES), jnp.float32),
            pltpu.SemaphoreType.DMA((NCHUNK + 2,)),
        ]
        + [pltpu.VMEM((lists, width), jnp.float32)] * NACC,
        compiler_params=pltpu.CompilerParams(vmem_limit_bytes=K1LIM),
        name="list_sums",
    )(core, ids, idv, x)


def code_counts_kernel(codes_ref, out_ref):
    subs, rows = codes_ref.shape
    digit = lax.broadcasted_iota(jnp.int32, (SUB_DIM, CBLOCK), 0)
    cc = jnp.zeros((LANES, LANES), jnp.float32)
    for b in range(0, rows, CBLOCK):
        left, right = [], []
        for m in range(subs):
            code = codes_ref[m : m + 1, b : b + CBLOCK]
            left.append((lax.shift_right_logical(code, 4) == digit).astype(jnp.bfloat16))
            right.append(((code & (SUB_DIM - 1)) == digit).astype(jnp.bfloat16))
        cc += lax.dot_general(
            jnp.concatenate(left, 0), jnp.concatenate(right, 0), NT, preferred_element_type=jnp.float32
        )
    r = lax.broadcasted_iota(jnp.int32, cc.shape, 0) // SUB_DIM
    c = lax.broadcasted_iota(jnp.int32, cc.shape, 1) // SUB_DIM
    cc = jnp.where(r == c, cc, 0.0)
    total = cc[0:SUB_DIM, :]
    for m in range(1, subs):
        total = total + cc[m * SUB_DIM : (m + 1) * SUB_DIM, :]
    out_ref[...] = total


def code_counts(codes_t):
    vmem = pl.BlockSpec(memory_space=pltpu.VMEM)
    return pl.pallas_call(
        code_counts_kernel,
        in_specs=[vmem],
        out_specs=vmem,
        out_shape=jax.ShapeDtypeStruct((SUB_DIM, LANES), jnp.float32),
        compiler_params=pltpu.CompilerParams(vmem_limit_bytes=8 * 2**20),
        cost_estimate=pl.CostEstimate(flops=10**9, bytes_accessed=4 * 10**6, transcendentals=0),
        name="code_counts",
    )(codes_t)


def centroid_kernel(prior, part_ref, old_ref, cent_ref, copies_ref):
    owned = old_ref.shape[0]
    total = part_ref[0]
    for k in range(1, part_ref.shape[0]):
        total = total + part_ref[k]
    eye = (
        lax.broadcasted_iota(jnp.int32, (LANES, LANES), 0)
        == lax.broadcasted_iota(jnp.int32, (LANES, LANES), 1)
    )
    for h in range(owned // LANES):
        row = total[owned + h : owned + h + 1, :]
        col = jnp.sum(jnp.where(eye, row, 0.0), axis=1, keepdims=True)
        sl = slice(h * LANES, (h + 1) * LANES)
        cent = (total[sl, :] + prior * old_ref[sl, :]) / (col + prior)
        cent_ref[sl, :] = cent
        for k in range(copies_ref.shape[0]):
            copies_ref[k, sl, :] = cent


def new_centroids(parts, old, prior):
    n = parts.shape[0]
    return pl.pallas_call(
        functools.partial(centroid_kernel, prior),
        out_shape=[
            jax.ShapeDtypeStruct(old.shape, jnp.float32),
            jax.ShapeDtypeStruct((n,) + old.shape, jnp.float32),
        ],
        compiler_params=pltpu.CompilerParams(vmem_limit_bytes=16 * 2**20),
        name="centroids",
    )(parts, old)


NT = (((1,), (1,)), ((), ()))


def resid_kernel(
    core_ref, row_ref, ids_ref, codes_ref, x_ref, own_ref, other_ref, counts_ref, old_ref, rest_ref, keep_ref, send_ref, ids, table, got0, got1, sumst, tall, sems, *, prior
):
    block = got0.shape[0]
    rows = x_ref.shape[0]
    pieces, owned, _ = own_ref.shape
    subs = codes_ref.shape[0]
    owners = counts_ref.shape[0]
    each = old_ref.shape[0]
    half = owners * each // 2
    early, late = pl.ds(0, 2 * block), pl.ds(2 * block, rows - 2 * block)
    fetch = [pltpu.make_async_copy(ids_ref.at[p], ids.at[p], sems.at[n]) for n, p in enumerate((early, late))]
    for f in fetch:
        f.start()
    core = core_ref[0]
    for k in range(pieces):
        table[pl.ds(pl.multiple_of((2 * k + core) * owned, owned), owned), :] = own_ref[k]
        table[pl.ds(pl.multiple_of((2 * k + 1 - core) * owned, owned), owned), :] = other_ref[k]
    sumst[...] = jnp.zeros_like(sumst)
    fetch[0].wait()

    sublane = lax.broadcasted_iota(jnp.int32, (8, LANES), 0)

    def gather(start, got):
        for g in range(0, block, 8):
            tile = None
            for j in range(8):
                row = ids.at[pl.ds(g + j, rows - block + 1)][start]
                line = jnp.broadcast_to(table[pl.ds(row, 1), :], (8, LANES))
                tile = line if j == 0 else jnp.where(sublane == j, line, tile)
            got[g : g + 8, :] = tile

    def work(start, got):
        here = pl.ds(start, block)
        rest = (x_ref[here, :] - got[...]).T
        rest_ref[:, here] = rest
        hi = rest.astype(jnp.bfloat16)
        lo = (rest - hi.astype(jnp.float32)).astype(jnp.bfloat16)
        label = lax.broadcasted_iota(jnp.int32, (half, block), 0)
        for p in range(subs // 2):
            left, right = [], []
            for m in (2 * p, 2 * p + 1):
                code = codes_ref[pl.ds(m, 1), here]
                right.append(((code & (half - 1)) == label).astype(jnp.bfloat16))
                f = slice(m * SUB_DIM, (m + 1) * SUB_DIM)
                both = jnp.concatenate([hi[f], lo[f]], 0)
                top = jnp.broadcast_to((code < half).astype(jnp.bfloat16), both.shape)
                first = both * top
                left += [first, both - first]
            part = lax.dot_general(
                jnp.concatenate(left, 0), jnp.concatenate(right, 0), NT, preferred_element_type=jnp.float32
            )
            for s in range(2):
                f = slice((2 * p + s) * SUB_DIM, (2 * p + s + 1) * SUB_DIM)
                for h in range(2):
                    band = part[(4 * s + 2 * h) * SUB_DIM : (4 * s + 2 * h + 2) * SUB_DIM, s * half : (s + 1) * half]
                    sumst[f, h * half : (h + 1) * half] += band[:SUB_DIM] + band[SUB_DIM:]

    gather(0, got0)
    fetch[1].wait()

    @pl.loop(0, rows // (UNROLL * block))
    def _(i):
        base = pl.multiple_of(i * UNROLL * block, block)
        for u in range(UNROLL):
            now, after = (got0, got1) if u % 2 == 0 else (got1, got0)
            here = pl.multiple_of(base + u * block, block)
            gather(pl.multiple_of(jnp.minimum(here + block, rows - block), block), after)
            work(here, now)

    tall[...] = sumst[...].T
    mine = pl.ds(pl.multiple_of(row_ref[0] * each, each), each)
    tall[mine, :] += prior * old_ref[...]
    for out, parity in ((keep_ref, core), (send_ref, 1 - core)):
        for k in range(owners // 2):
            o = 2 * k + parity
            out[k * each : (k + 1) * each, :] = tall[pl.ds(pl.multiple_of(o * each, each), each), :]
            out[pl.ds(owners // 2 * each + k, 1), :] = counts_ref[pl.ds(o, 1), :]


def residuals(core, row, ids, codes_t, x, own, other, counts, old, owners, prior, block=RBLOCK):
    codes = owners * old.shape[0]
    half = jax.ShapeDtypeStruct((codes // 2 + owners // 2, x.shape[1]), jnp.float32)
    rows, width = x.shape
    pieces, owned, _ = own.shape
    vmem = pl.BlockSpec(memory_space=pltpu.VMEM)
    return pl.pallas_call(
        functools.partial(resid_kernel, prior=prior),
        in_specs=[pl.BlockSpec(memory_space=pltpu.SMEM)] * 2 + [vmem] * 7,
        out_specs=[vmem] * 3,
        out_shape=[
            jax.ShapeDtypeStruct((width, rows), jnp.float32),
            half,
            half,
        ],
        scratch_shapes=[
            pltpu.SMEM((rows,), jnp.int32),
            pltpu.VMEM((2 * pieces * owned, width), jnp.float32),
            pltpu.VMEM((block, width), jnp.float32),
            pltpu.VMEM((block, width), jnp.float32),
            pltpu.VMEM((width, codes), jnp.float32),
            pltpu.VMEM((codes, width), jnp.float32),
            pltpu.SemaphoreType.DMA((2,)),
        ],
        compiler_params=pltpu.CompilerParams(vmem_limit_bytes=VLIM),
        name="residuals",
    )(core, row, ids, codes_t, x, own, other, counts, old)


def book_bands(book_t, pair):
    half = book_t.shape[1] // 2
    bands = []
    for s in range(2):
        f = slice((2 * pair + s) * SUB_DIM, (2 * pair + s + 1) * SUB_DIM)
        for h in range(2):
            words = book_t[f, h * half : (h + 1) * half]
            hi = words.astype(jnp.bfloat16)
            lo = (words - hi.astype(jnp.float32)).astype(jnp.bfloat16)
            none = jnp.zeros_like(hi)
            bands += [jnp.concatenate([p, none] if s == 0 else [none, p], 1) for p in (hi, lo)]
    return jnp.concatenate(bands, 0)


def whole_book(prior, core_ref, own_ref, other_ref, each, book_ref, counts_ref):
    owners = book_ref.shape[0] // each
    core = core_ref[0]
    for src, parity in ((own_ref, core), (other_ref, 1 - core)):
        for k in range(owners // 2):
            o = 2 * k + parity
            book_ref[pl.ds(pl.multiple_of(o * each, each), each), :] = src[k * each : (k + 1) * each, :]
            counts_ref[pl.ds(o, 1), :] = src[pl.ds(owners // 2 * each + k, 1), :]
    lane = lax.broadcasted_iota(jnp.int32, (each, LANES), 1)
    code = lax.broadcasted_iota(jnp.int32, (each, LANES), 0)
    keep = (lane & (SUB_DIM - 1)) == code
    whole = counts_ref[...].astype(jnp.int32)
    digits = [lax.shift_right_logical(whole, 12), lax.shift_right_logical(whole, 6) & 63, whole & 63]
    picked = jnp.concatenate(
        [
            jnp.concatenate([jnp.where(keep, d[o : o + 1, :], 0) for o in range(owners)], 0).astype(jnp.bfloat16)
            for d in digits
        ],
        1,
    )
    r = lax.broadcasted_iota(jnp.int32, (LANES, LANES), 0) // SUB_DIM
    c = lax.broadcasted_iota(jnp.int32, (LANES, LANES), 1) // SUB_DIM
    ones = jnp.concatenate([jnp.where(r == c, w, 0.0).astype(jnp.bfloat16) for w in (4096.0, 64.0, 1.0)], 0)
    spread = jnp.dot(picked, ones, preferred_element_type=jnp.float32)
    book_ref[...] = book_ref[...] / (spread + prior)


def errors_kernel(core_ref, row_ref, own_ref, other_ref, codes_ref, rest_ref, out_ref, mine_ref, table, bands, book_ref, counts_ref, *, prior):
    subs, rows = codes_ref.shape
    half = book_ref.shape[0] // 2
    each = mine_ref.shape[0]
    whole_book(prior, core_ref, own_ref, other_ref, each, book_ref, counts_ref)
    mine_ref[...] = book_ref[pl.ds(pl.multiple_of(row_ref[0] * each, each), each), :]
    by_product = bands.shape[0]
    looked_up = subs - 2 * by_product

    table[...] = book_ref[...].T
    for q in range(by_product):
        bands[q] = book_bands(table[...], looked_up // 2 + q)
    label = lax.broadcasted_iota(jnp.int32, (half, EBLOCK), 0)

    def product(here):
        acc = jnp.zeros((8, EBLOCK), jnp.float32)
        for q in range(by_product):
            m0 = looked_up + 2 * q
            code = [codes_ref[m : m + 1, here] for m in (m0, m0 + 1)]
            hot = [((c & (half - 1)) == label).astype(jnp.bfloat16) for c in code]
            part = jnp.dot(bands[q], jnp.concatenate(hot, 0), preferred_element_type=jnp.float32)
            for s in range(2):
                p = [part[(4 * s + b) * SUB_DIM : (4 * s + b + 1) * SUB_DIM, :] for b in range(4)]
                word = jnp.where(jnp.broadcast_to(code[s] < half, p[0].shape), p[0] + p[1], p[2] + p[3])
                d = rest_ref[(m0 + s) * SUB_DIM : (m0 + s + 1) * SUB_DIM, here] - word
                d = d * d
                for g in range(0, SUB_DIM, 8):
                    acc = acc + d[g : g + 8, :]
        return acc

    def lookup(cols):
        acc = jnp.zeros((8, LANES), jnp.float32)
        for m in range(looked_up):
            idx = jnp.broadcast_to(codes_ref[m : m + 1, cols], (8, LANES))
            low = idx & (half - 1)
            first = idx < half
            for g in range(0, SUB_DIM, 8):
                f = slice(m * SUB_DIM + g, m * SUB_DIM + g + 8)
                a = jnp.take_along_axis(table[f, 0:half], low, axis=1)
                b = jnp.take_along_axis(table[f, half : 2 * half], low, axis=1)
                d = rest_ref[f, cols] - jnp.where(first, a, b)
                acc = acc + d * d
        return acc

    for b in range(0, rows, EBLOCK):
        wide = product(slice(b, b + EBLOCK))
        for t in range(0, EBLOCK, LANES):
            acc = wide[:, t : t + LANES] + lookup(slice(b + t, b + t + LANES))
            row = jnp.sum(acc, axis=0, keepdims=True)
            at = (b + t) // LANES
            for k in range(out_ref.shape[0]):
                out_ref[k, at : at + 1, :] = row


def errors(core, row, own, other, codes_t, rest, copies, owned, owners, prior):
    width, rows = rest.shape
    codes = owned * owners
    vmem = pl.BlockSpec(memory_space=pltpu.VMEM)
    return pl.pallas_call(
        functools.partial(errors_kernel, prior=prior),
        in_specs=[pl.BlockSpec(memory_space=pltpu.SMEM)] * 2 + [vmem] * 4,
        out_specs=[vmem] * 2,
        out_shape=[
            jax.ShapeDtypeStruct((copies, rows // LANES, LANES), jnp.float32),
            jax.ShapeDtypeStruct((owned, width), jnp.float32),
        ],
        scratch_shapes=[
            pltpu.VMEM((width, codes), jnp.float32),
            pltpu.VMEM((EPAIRS, LANES, codes), jnp.bfloat16),
            pltpu.VMEM((codes, width), jnp.float32),
            pltpu.VMEM((owners, width), jnp.float32),
        ],
        compiler_params=pltpu.CompilerParams(vmem_limit_bytes=24 * 2**20),
        name="errors",
    )(core, row, own, other, codes_t, rest)


def swap(x, axis, n, bit):
    return lax.ppermute(x, axis, [(i, i ^ bit) for i in range(n)])


def turned(x, axis, n, ring, step):
    def there(i):
        y, at, core = i // (2 * ring), i // 2 % ring, i % 2
        return (y * ring + (at + step) % ring) * 2 + core

    return lax.ppermute(x, axis, [(i, there(i)) for i in range(n)])


def local(passages, list_ids, code_ids, old_centroids, old_codebook):
    rows, width = passages.shape
    n_row = lax.axis_size("row")
    n_col = lax.axis_size("col")
    total = rows * n_row
    owned_lists = old_centroids.shape[0]
    owned_codes = old_codebook.shape[0]
    lists = owned_lists * n_row
    codes = owned_codes * n_row
    list_prior = float(total // lists)
    code_prior = float(total // codes)
    pieces = n_row // 2
    same_core = [[2 * k + c for k in range(pieces)] for c in range(2)]
    row = lax.axis_index("row").astype(jnp.int32).reshape(1)
    core = (lax.axis_index("row") % 2).astype(jnp.int32).reshape(1)
    codes_t = code_ids.T

    keep, send = list_sums(core, list_ids, passages, pieces, lists)
    pair = keep + swap(send, "row", n_row, 1)
    parts = lax.all_to_all(pair, "row", 0, 0, axis_index_groups=same_core, tiled=True)
    centroids, copies = new_centroids(parts, old_centroids, list_prior)
    own = lax.all_to_all(copies, "row", 0, 0, axis_index_groups=same_core, tiled=True)
    other = swap(own, "row", n_row, 1)
    rest, keep, send = residuals(
        core, row, list_ids, codes_t, passages, own, other, code_counts(codes_t), old_codebook, n_row, code_prior
    )
    far = n_row // 2
    half = keep + swap(send, "row", n_row, 1) + swap(keep, "row", n_row, far) + swap(send, "row", n_row, far + 1)
    ring = n_row // 4
    half = half + sum(turned(half, "row", n_row, ring, step) for step in range(1, ring))
    err, codebook = errors(
        core, row, half, swap(half, "row", n_row, 1), codes_t, rest, n_col, owned_codes, n_row, code_prior
    )
    err = lax.all_to_all(err, "col", 0, 0, tiled=True)
    return centroids, codebook, jnp.sum(err, axis=0).reshape(rows) / D


def solution(mesh):
    in_specs = (P("row", "col"), P("row"), P("row", "col"), P("row", "col"), P("row", "col"))
    out_specs = (P("row", "col"), P("row", "col"), P("row"))
    return jax.shard_map(local, mesh=mesh, in_specs=in_specs, out_specs=out_specs, check_vma=False)
```
